32 devices in a mesh: dp: 8 (over y, x, core), tensor: 4 (over z).
Axes of the slice: x: 2, y: 2, z: 4, core: 2. Of those that a mesh axis runs over, the one named last changes fastest.
Arguments:
- hidden_in: float32 [16384, 1024], P(('dp', 'tensor')), may hold values from -6 to 6
- ln1_gain: bfloat16 [1024], P(('dp', 'tensor')), may hold values from 0.25 to 1.75
- ln1_bias: bfloat16 [1024], P(('dp', 'tensor')), may hold values from -3 to 3
- qkv_weight: bfloat16 [1024, 3072], P('dp', 'tensor'), may hold values from -0.1875 to 0.1875
- qkv_bias: bfloat16 [16, 128], P('tensor', 'dp'), may hold values from -3 to 3
- out_weight: bfloat16 [1024, 1024], P('tensor', 'dp'), may hold values from -0.75 to 0.75
- out_bias: bfloat16 [1024], P(('dp', 'tensor')), may hold values from -3 to 3
- ln2_gain: bfloat16 [1024], P(('dp', 'tensor')), may hold values from 0.25 to 1.75
- ln2_bias: bfloat16 [1024], P(('dp', 'tensor')), may hold values from -3 to 3
- up_weight: bfloat16 [1024, 4096], P('dp', 'tensor'), may hold values from -0.1875 to 0.1875
- up_bias: bfloat16 [16, 256], P('tensor', 'dp'), may hold values from -3 to 3
- down_weight: bfloat16 [4096, 1024], P('tensor', 'dp'), may hold values from -0.09375 to 0.09375
- down_bias: bfloat16 [1024], P(('dp', 'tensor')), may hold values from -3 to 3
- cotangent: float32 [16384, 1024], P(('dp', 'tensor')), may hold values from -6 to 6
Outputs:
- output: float32 [16384, 1024], P(('dp', 'tensor'))
- grad_in: float32 [16384, 1024], P(('dp', 'tensor'))
- grad_ln1_gain: float32 [1024], P(('dp', 'tensor'))
- grad_ln1_bias: float32 [1024], P(('dp', 'tensor'))
- grad_qkv_weight: float32 [1024, 3072], P('dp', 'tensor')
- grad_qkv_bias: float32 [16, 128], P('tensor', 'dp')
- grad_out_weight: float32 [1024, 1024], P('tensor', 'dp')
- grad_out_bias: float32 [1024], P(('dp', 'tensor'))
- grad_ln2_gain: float32 [1024], P(('dp', 'tensor'))
- grad_ln2_bias: float32 [1024], P(('dp', 'tensor'))
- grad_up_weight: float32 [1024, 4096], P('dp', 'tensor')
- grad_up_bias: float32 [16, 256], P('tensor', 'dp')
- grad_down_weight: float32 [4096, 1024], P('tensor', 'dp')
- grad_down_bias: float32 [1024], P(('dp', 'tensor'))
The draws below stay inside these ranges and needn't reach their ends.
All inputs are finite; a program needn't handle non-finite values.
Results may differ from the reference program's by a relative error of at most 0.023.
Values may be sent and summed in bfloat16 or wider, within the bound.
No kernel may reach another device: no remote copies, remote signals or barrier semaphores. Data moves between devices by JAX's collectives and lax.ppermute only.
A program may use at most 128 MiB of HBM per device.

```python
from functools import partial
import jax
import jax.numpy as jnp
from jax import lax

D = 1024
H = 16
HD = 64
FF = 4096
SEQ_LEN = 1024
SEQ_DP = 2
TOKENS = 16384
N_DP = 8


def strengthened(result, rng, source, target, blocks, factor):
    def block_of(dim):
        return (jnp.arange(result.shape[dim]) // (result.shape[dim] // blocks)).reshape((-1,) + (1,) * (result.ndim - 1 - dim))

    first = jax.random.permutation(rng, blocks)[block_of(target)]
    far = (block_of(target) + blocks // 2) % blocks
    return jnp.where((block_of(source) == first) | (block_of(source) == far), factor * result, result)


def block_levels(key, extent, cuts, smallest, largest):
    def one(axis_at, shards_of):
        steps = jax.random.uniform(jax.random.fold_in(jax.random.fold_in(key, 6), axis_at), (shards_of,), jnp.float32, smallest / len(cuts), largest / len(cuts))
        return jnp.repeat(jnp.exp(steps), extent[axis_at] // shards_of).reshape((-1,) + (1,) * (len(extent) - axis_at - 1))

    loudness = one(*cuts[0])
    for cut in cuts[1:]:
        loudness = loudness * one(*cut)
    return loudness


def normal_values(own_key, extent, deviation, bound, shards=(), kind=jnp.bfloat16):
    array = jax.random.normal(own_key, extent, jnp.float32) * deviation
    if len(shards) > 0:
        array = block_levels(own_key, extent, shards, -0.22, 0.18) * array
    return jnp.clip(array, min=-bound, max=bound).astype(kind)


def heavy_noise(stream_key, extent, scale, bound, split, heavy, kind=jnp.bfloat16):
    values = scale * jax.random.normal(stream_key, extent, jnp.float32)
    if split:
        values = values * block_levels(stream_key, extent, split, -0.22, 0.18)
    return jnp.clip(strengthened(values, jax.random.fold_in(stream_key, 3), *heavy), -bound, bound).astype(kind)


def setup_inputs(seed: int = 0) -> dict:
    keys = jax.random.split(jax.random.key(seed), 15)
    hidden_in = normal_values(keys[0], (TOKENS, D), 1.0, 6.0, ((0, 32),), jnp.float32)
    ln1_gain = jnp.clip(1.0 + 0.15 * jax.random.normal(keys[1], (D,), jnp.float32), 0.25, 1.75).astype(jnp.bfloat16)
    ln1_bias = normal_values(keys[2], (D,), 0.5, 3.0, ((0, 32),))
    qkv_weight = normal_values(keys[3], (D, 3 * D), D ** -0.5, 0.1875, ((0, 8), (1, 4)))
    qkv_bias = normal_values(keys[4], (H, 2 * HD), 0.5, 3.0, ((0, 4), (1, 8)))
    out_weight = normal_values(keys[5], (D, D), (D // 16) ** -0.5, 0.75, ((0, 4), (1, 8)))
    out_bias = normal_values(keys[6], (D,), 0.5, 3.0, ((0, 32),))
    ln2_gain = jnp.clip(1.0 + 0.15 * jax.random.normal(keys[7], (D,), jnp.float32), 0.25, 1.75).astype(jnp.bfloat16)
    ln2_bias = normal_values(keys[8], (D,), 0.5, 3.0, ((0, 32),))
    up_weight = normal_values(keys[9], (D, FF), D ** -0.5, 0.1875, ((0, 8), (1, 4)))
    up_bias = normal_values(keys[10], (H, FF // H), 0.5, 3.0, ((0, 4), (1, 8)))
    down_weight = normal_values(keys[11], (FF, D), FF ** -0.5, 0.09375, ((0, 4), (1, 8)))
    down_bias = normal_values(keys[12], (D,), 0.5, 3.0, ((0, 32),))
    cotangent = heavy_noise(keys[13], (TOKENS, D), 1.0, 6.0, ((0, 32),), (0, 1, 32, 2.75), jnp.float32)
    return {"hidden_in": hidden_in, "ln1_gain": ln1_gain, "ln1_bias": ln1_bias, "qkv_weight": qkv_weight, "qkv_bias": qkv_bias, "out_weight": out_weight, "out_bias": out_bias, "ln2_gain": ln2_gain, "ln2_bias": ln2_bias, "up_weight": up_weight, "up_bias": up_bias, "down_weight": down_weight, "down_bias": down_bias, "cotangent": cotangent}


@jax.custom_vjp
def low(v):
    return lax.optimization_barrier(v.astype(jnp.bfloat16)).astype(jnp.float32)

@jax.custom_vjp
def low_back(v):
    return v

def low_keep(v):
    return (low(v), None)

def low_pass(kept, grad):
    return (grad,)

def back_keep(v):
    return (v, None)

def back_low(kept, grad):
    return (low(grad),)
low.defvjp(low_keep, low_pass)
low_back.defvjp(back_keep, back_low)
EPSILON = 1e-05
MASKED = -1e+30
HIGH = lax.Precision.HIGHEST

def layer_norm(values, gain, shift):
    mean_row = lax.optimization_barrier(jnp.mean(values, axis=-1, keepdims=True))
    centred = values - mean_row
    spread = lax.optimization_barrier(jnp.mean(centred * centred, axis=-1, keepdims=True))
    return centred * lax.rsqrt(spread + EPSILON) * gain + shift

def gelu_tanh(values):
    inner = 0.7978845608028654 * (values + 0.044715 * values * values * values)
    return 0.5 * values * (1.0 + jnp.tanh(inner))

def attend(seq_parts, slopes):
    queries, keys_all, values_all = seq_parts
    positions = jnp.arange(SEQ_LEN)
    offset = (positions[None, :] - positions[:, None]).astype(jnp.float32)
    raw_scores = jnp.einsum('qhe,khe->hqk', queries, keys_all, precision=HIGH)
    scores = low_back(raw_scores * HD ** (-0.5) + slopes[:, None, None] * offset[None])
    scores = jnp.where((positions[None, :] <= positions[:, None])[None], scores, MASKED)
    row_max = lax.optimization_barrier(jnp.max(scores, axis=2, keepdims=True))
    exp_scores = jnp.exp(scores - row_max)
    attn_probs = low(exp_scores / lax.optimization_barrier(jnp.sum(exp_scores, axis=2, keepdims=True)))
    return jnp.einsum('hqk,khe->qhe', attn_probs, values_all, precision=HIGH)

def layer_group(hidden, params):
    ln1_gain, ln1_bias, qkv_weight, qkv_bias, out_weight, out_bias, ln2_gain, ln2_bias, up_weight, up_bias, down_weight, down_bias = params
    normed_one = low(layer_norm(hidden, ln1_gain, ln1_bias))
    bias_full = jnp.concatenate([qkv_bias[:, :HD], jnp.zeros((H, HD), qkv_bias.dtype), qkv_bias[:, HD:]], axis=1).reshape(3 * D)
    qkv_full = low(low_back(jnp.dot(normed_one, qkv_weight, precision=HIGH) + bias_full))
    qkv_split = qkv_full.reshape(SEQ_DP, SEQ_LEN, H, 3, HD)
    slopes = jnp.exp2(-8.0 * (jnp.arange(H) + 1).astype(jnp.float32) / H)
    attended = lax.map(jax.checkpoint(partial(attend, slopes=slopes)), (qkv_split[:, :, :, 0], qkv_split[:, :, :, 1], qkv_split[:, :, :, 2]))
    context = low(low_back(attended.reshape(SEQ_DP * SEQ_LEN, D)))
    residual_mid = hidden + (low_back(jnp.dot(context, out_weight, precision=HIGH)) + out_bias)
    normed_two = low(layer_norm(residual_mid, ln2_gain, ln2_bias))
    up_pre = low_back(jnp.dot(normed_two, up_weight, precision=HIGH) + up_bias.reshape(FF))
    active = low(gelu_tanh(up_pre))
    return residual_mid + (low_back(jnp.dot(active, down_weight, precision=HIGH)) + down_bias)

def forward(hidden, params):
    grouped = hidden.reshape(N_DP, SEQ_DP * SEQ_LEN, D)
    outcome = lax.map(jax.checkpoint(partial(layer_group, params=params)), grouped)
    return outcome.reshape(N_DP * SEQ_DP * SEQ_LEN, D)

def reference(hidden_in, ln1_gain, ln1_bias, qkv_weight, qkv_bias, out_weight, out_bias, ln2_gain, ln2_bias, up_weight, up_bias, down_weight, down_bias, cotangent):
    params = jax.tree.map(lambda tensor_arg: tensor_arg.astype(jnp.float32), (ln1_gain, ln1_bias, qkv_weight, qkv_bias, out_weight, out_bias, ln2_gain, ln2_bias, up_weight, up_bias, down_weight, down_bias))
    output, pullback = jax.vjp(forward, hidden_in.astype(jnp.float32), params)
    grad_in, grads = pullback(cotangent.astype(jnp.float32))
    return (output, grad_in, grads[0], grads[1], grads[2], grads[3], grads[4], grads[5], grads[6], grads[7], grads[8], grads[9], grads[10], grads[11])
```

```python
import functools

import jax
import jax.numpy as jnp
from jax import lax
from jax.experimental import pallas as pl
from jax.experimental.pallas import tpu as pltpu
from jax.sharding import PartitionSpec as P

H = 16
HD = 64
FF = 4096
SEQ_LEN = 1024
EPSILON = 1e-05
MASKED = -1e30
BF = jnp.bfloat16
F32 = jnp.float32


def gelu_tanh(values):
    inner = 0.7978845608028654 * (values + 0.044715 * values * values * values)
    return 0.5 * values * (1.0 + jnp.tanh(inner))


def dot_nn(left, right):
    return lax.dot_general(left, right, (((1,), (0,)), ((), ())), preferred_element_type=F32)


def dot_tn(left, right):
    return lax.dot_general(left, right, (((0,), (0,)), ((), ())), preferred_element_type=F32)


def dot_nt(left, right):
    return lax.dot_general(left, right, (((1,), (1,)), ((), ())), preferred_element_type=F32)


def swap_bit(values, bit):
    size = lax.axis_size("dp")
    return lax.ppermute(values, "dp", [(i, i ^ (1 << bit)) for i in range(size)])


def swap_core(values):
    return swap_bit(values, 0)


def from_tensor(values, step):
    size = lax.axis_size("tensor")
    return lax.ppermute(values, "tensor", [(i, (i - step) % size) for i in range(size)])


def swap_pair(values):
    dp, tensor = lax.axis_size("dp"), lax.axis_size("tensor")
    pairs = []
    for d in range(dp):
        for t in range(tensor):
            if d % 2 != t % 2:
                pairs.append((d * tensor + t, (d ^ 1) * tensor + (t ^ 1)))
    return lax.ppermute(values, ("dp", "tensor"), pairs)


def chip_bits():
    return (lax.axis_size("dp") // 2).bit_length() - 1


def gather_chips(line, split):
    bits = chip_bits()
    if bits == 2:
        along = swap_bit(line, 1)
        across = swap_bit(line, 2)
        far_top = swap_bit(along[:split], 2)
        far_low = swap_bit(across[split:], 1)
        return [
            [line[:split], line[split:]],
            [along[:split], along[split:]],
            [across[:split], across[split:]],
            [far_top, far_low],
        ]
    held = line[None]
    for bit in range(bits):
        held = jnp.concatenate([held, swap_bit(held, bit + 1)], axis=0)
    return [[held[r, :split], held[r, split:]] for r in range(1 << bits)]


def scatter_chips(grad, rows, split):
    bits = chip_bits()
    if bits == 2:
        block = [grad[r * rows : (r + 1) * rows] for r in range(4)]
        far_top = swap_bit(block[3][:split], 2)
        far_low = swap_bit(block[3][split:], 1)
        top = (block[1][:split].astype(F32) + far_top.astype(F32)).astype(BF)
        low = (block[2][split:].astype(F32) + far_low.astype(F32)).astype(BF)
        along = swap_bit(jnp.concatenate([top, block[1][split:]], axis=0), 1)
        across = swap_bit(jnp.concatenate([block[2][:split], low], axis=0), 2)
        return block[0].astype(F32) + along.astype(F32) + across.astype(F32)
    held = grad.reshape(-1, rows, grad.shape[1])
    for bit in range(bits)[::-1]:
        half = held.shape[0] // 2
        got = swap_bit(held[half:], bit + 1)
        held = (held[:half].astype(F32) + got.astype(F32)).astype(BF)
    return held[0].astype(F32)


def gather_weights(piece, widths, extra=None):
    size = lax.axis_size("tensor")
    rows = piece.shape[0]
    mine = piece if extra is None else jnp.concatenate([piece, extra], axis=0)
    turned = [mine] + [from_tensor(mine, k) for k in range(1, size)]
    cols, at = [], 0
    for width in widths:
        cols += [t[:rows, at : at + width] for t in turned]
        at += width
    line = jnp.concatenate(cols, axis=1)
    if extra is not None:
        added = functools.reduce(jnp.add, [t[rows:] for t in turned])
        added = jnp.pad(added, ((0, 0), (0, line.shape[1] - added.shape[1])))
        line = jnp.concatenate([line, added], axis=0)
    got = gather_chips(line, rows // 2)
    out, at = [], 0
    for width in widths:
        cut = slice(at, at + size * width)
        out.append(jnp.concatenate([part for top, low in got for part in (top[:, cut], low[: rows - rows // 2, cut])]))
        at += size * width
    table = None
    if extra is not None:
        table = jnp.stack([low[rows - rows // 2 :, : extra.shape[1]] for _, low in got])
    return out, table


def scatter_grads(grad, core):
    size = lax.axis_size("tensor")
    rows = grad.shape[0] // (lax.axis_size("dp") // 2)
    width = grad.shape[1] // size
    line = scatter_chips(grad, rows, rows // 2)
    total = line[:, :width]
    for k in range(1, size):
        part = line[:, k * width : (k + 1) * width].astype(BF)
        total = total + from_tensor(part, size - k).astype(F32)
    half = rows // 2
    keep = lax.dynamic_slice_in_dim(total, core * half, half, 0)
    give = lax.dynamic_slice_in_dim(total, (1 - core) * half, half, 0)
    got = swap_core(give)
    return jnp.where(core == 0, jnp.stack([keep, got], 1), jnp.stack([got, keep], 1))


def both_halves(mine, other, core):
    return jnp.concatenate([jnp.where(core == 0, mine, other), jnp.where(core == 0, other, mine)], axis=0)


def to_sequence(mine, core, keeps):
    here = jnp.where(keeps, mine, swap_pair(mine))
    return both_halves(here, swap_core(here), core)


def from_sequence(left, weight, core):
    half = left.shape[0] // 2
    give = lax.dynamic_slice_in_dim(left, (1 - core) * half, half, 0)
    got = swap_core(dot_nt(give, weight).astype(BF))
    own = dot_nt(lax.dynamic_slice_in_dim(left, core * half, half, 0), weight)
    here = (own + got.astype(F32)).astype(BF)
    return here, swap_pair(here)


BLOCK_Q = 256


def biased_pair(q, k, slope_ref, group, head):
    seq = k.shape[0]
    lane = lax.broadcasted_iota(jnp.int32, (1, 2 * HD), 1)
    mine = (lane >= head * HD) & (lane < (head + 1) * HD)
    slot = lane & (HD - 1)
    bias = slope_ref[group, head] * lax.broadcasted_iota(jnp.int32, (seq, 2 * HD), 0).astype(F32)
    high = bias.astype(BF)
    rest = bias - high.astype(F32)
    middle = rest.astype(BF)
    low = (rest - middle.astype(F32)).astype(BF)
    zero = jnp.zeros_like(k)
    extra = jnp.where(slot == 0, high, jnp.where(slot == 1, middle, jnp.where(slot == 2, low, zero)))
    ones = jnp.where(slot < 3, 1.0, 0.0).astype(BF)
    return jnp.where(mine, q, jnp.broadcast_to(ones, q.shape)), jnp.where(mine, k, extra), mine


def below_diagonal(size):
    keys = lax.broadcasted_iota(jnp.int32, (size, size), 0)
    return keys <= lax.broadcasted_iota(jnp.int32, (size, size), 1)


def attend_kernel(slope_ref, qkv_ref, ctx_ref, lse_ref):
    group = pl.program_id(0)
    wide = 2 * HD
    seq = qkv_ref.shape[0]
    size = min(BLOCK_Q, seq)
    q = qkv_ref[:, :wide] * BF(HD**-0.5)
    k = qkv_ref[:, wide : 2 * wide]
    v_t = qkv_ref[:, 2 * wide :].T
    heads = [biased_pair(q, k, slope_ref, group, h) for h in range(2)]
    seen = below_diagonal(size)
    for i in range(seq // size):
        lo, hi = i * size, (i + 1) * size
        outs = []
        for h, (qh, kh, _) in enumerate(heads):
            s = dot_nt(kh[:hi], qh[lo:hi])
            last = jnp.where(seen, s[lo:], MASKED)
            top = jnp.max(last, axis=0, keepdims=True)
            if i:
                top = jnp.maximum(top, jnp.max(s[:lo], axis=0, keepdims=True))
            e = jnp.exp(last - top)
            total = jnp.sum(e, axis=0, keepdims=True)
            e = e.astype(BF)
            if i:
                e0 = jnp.exp(s[:lo] - top)
                total = total + jnp.sum(e0, axis=0, keepdims=True)
                e = jnp.concatenate([e0.astype(BF), e], axis=0)
            o_t = dot_nn(v_t[h * HD : (h + 1) * HD, :hi], e)
            outs.append(o_t * (1.0 / total))
            lse_ref[0, h : h + 1, lo:hi] = top + jnp.log(total)
        ctx_ref[lo:hi, :] = jnp.concatenate(outs, axis=0).T.astype(BF)


def attend(qkv, slopes):
    seq, groups = qkv.shape[0], slopes.shape[0]
    wide = 2 * HD
    return pl.pallas_call(
        attend_kernel,
        grid=(groups,),
        in_specs=[
            pl.BlockSpec(memory_space=pltpu.SMEM),
            pl.BlockSpec((seq, 3 * wide), lambda g: (0, g)),
        ],
        out_specs=[
            pl.BlockSpec((seq, wide), lambda g: (0, g)),
            pl.BlockSpec((1, 2, seq), lambda g: (g, 0, 0)),
        ],
        out_shape=[
            jax.ShapeDtypeStruct((seq, groups * wide), BF),
            jax.ShapeDtypeStruct((groups, 2, seq), F32),
        ],
        compiler_params=pltpu.CompilerParams(vmem_limit_bytes=48 * 1024 * 1024),
        cost_estimate=pl.CostEstimate(
            flops=groups * 2 * seq * seq * HD * 4, bytes_accessed=qkv.size * 2 * 2, transcendentals=groups * seq * seq
        ),
        name="attend",
    )(slopes, qkv)


def attend_back_kernel(slope_ref, qkv_ref, grad_ref, lse_ref, out_ref, bias_ref, dk_ref, dv_ref):
    group = pl.program_id(0)
    wide = 2 * HD
    seq = qkv_ref.shape[0]
    size = min(BLOCK_Q, seq)
    q = qkv_ref[:, :wide] * BF(HD**-0.5)
    k = qkv_ref[:, wide : 2 * wide]
    v = qkv_ref[:, 2 * wide :]
    k_t = k.T
    zero = jnp.zeros_like(q)
    heads = [biased_pair(q, k, slope_ref, group, h) for h in range(2)]
    clean = [jnp.where(mine, q, zero) for _, _, mine in heads]
    grads = [jnp.where(mine, grad_ref[...], zero) for _, _, mine in heads]
    seen = below_diagonal(size)
    dk_ref[...] = jnp.zeros_like(dk_ref)
    dv_ref[...] = jnp.zeros_like(dv_ref)
    bias_q = jnp.zeros((1, wide), F32)
    for i in range(seq // size):
        lo, hi = i * size, (i + 1) * size
        outs = []
        for h, (qh, kh, _) in enumerate(heads):
            s = dot_nt(kh[:hi], qh[lo:hi])
            lse = lse_ref[0, h : h + 1, lo:hi]
            p = jnp.exp(jnp.where(seen, s[lo:], MASKED) - lse)
            if i:
                p = jnp.concatenate([jnp.exp(s[:lo] - lse), p], axis=0)
            dp = dot_nt(v[:hi], grads[h][lo:hi])
            inner = jnp.sum(p * dp, axis=0, keepdims=True)
            ds = (p * (dp - inner)).astype(BF)
            dk_ref[:hi, :] += dot_nn(ds, clean[h][lo:hi])
            dv_ref[:hi, :] += dot_nn(p.astype(BF), grads[h][lo:hi])
            outs.append(dot_nn(k_t[h * HD : (h + 1) * HD, :hi], ds))
        dq = (jnp.concatenate(outs, axis=0).T * HD**-0.5).astype(BF)
        bias_q = bias_q + jnp.sum(dq.astype(F32), axis=0, keepdims=True)
        out_ref[lo:hi, :wide] = dq
    dk = dk_ref[...].astype(BF)
    out_ref[:, wide : 2 * wide] = dk
    dv = dv_ref[...].astype(BF)
    out_ref[:, 2 * wide :] = dv
    bias_ref[0, :, :wide] = bias_q
    bias_ref[0, :, wide : 2 * wide] = jnp.sum(dk.astype(F32), axis=0, keepdims=True)
    bias_ref[0, :, 2 * wide :] = jnp.sum(dv.astype(F32), axis=0, keepdims=True)


def attend_back(qkv, slopes, lse, grad_ctx):
    seq, groups = qkv.shape[0], slopes.shape[0]
    wide = 2 * HD
    return pl.pallas_call(
        attend_back_kernel,
        grid=(groups,),
        in_specs=[
            pl.BlockSpec(memory_space=pltpu.SMEM),
            pl.BlockSpec((seq, 3 * wide), lambda g: (0, g)),
            pl.BlockSpec((seq, wide), lambda g: (0, g)),
            pl.BlockSpec((1, 2, seq), lambda g: (g, 0, 0)),
        ],
        out_specs=[
            pl.BlockSpec((seq, 3 * wide), lambda g: (0, g)),
            pl.BlockSpec((1, 1, 3 * wide), lambda g: (g, 0, 0)),
        ],
        out_shape=[
            jax.ShapeDtypeStruct(qkv.shape, BF),
            jax.ShapeDtypeStruct((groups, 1, 3 * wide), F32),
        ],
        scratch_shapes=[pltpu.VMEM((seq, wide), F32), pltpu.VMEM((seq, wide), F32)],
        compiler_params=pltpu.CompilerParams(vmem_limit_bytes=48 * 1024 * 1024),
        cost_estimate=pl.CostEstimate(
            flops=groups * 2 * seq * seq * HD * 10, bytes_accessed=qkv.size * 2 * 3, transcendentals=groups * seq * seq
        ),
        name="attend_back",
    )(slopes, qkv, grad_ctx, lse)


VMEM_LIMIT = 48 * 1024 * 1024


def read_mixed(ref, ids_ref, chips, mixed):
    if not mixed:
        return ref[...]
    block = ref.shape[1] // chips
    parts = [ref[:, pl.ds(pl.multiple_of((ids_ref[0] ^ r) * block, block), block)] for r in range(chips)]
    return jnp.concatenate(parts, axis=1)


def write_mixed(ref, values, ids_ref, chips, mixed):
    if not mixed:
        ref[...] = values
        return
    block = ref.shape[1] // chips
    for r in range(chips):
        ref[:, pl.ds(pl.multiple_of((ids_ref[0] ^ r) * block, block), block)] = values[:, r * block : (r + 1) * block]


def centre(x):
    mean_row = jnp.mean(x, axis=1, keepdims=True)
    centred = x - mean_row
    inv = lax.rsqrt(jnp.mean(centred * centred, axis=1, keepdims=True) + EPSILON)
    return centred * inv, inv


def norm_back(grad, gain, z, inv):
    g = grad * gain
    mean_g = jnp.mean(g, axis=1, keepdims=True)
    mean_gz = jnp.mean(g * z, axis=1, keepdims=True)
    return inv * (g - mean_g - z * mean_gz)


def add_sums(ref, rows):
    @pl.when(pl.program_id(0) == 0)
    def _():
        ref[...] = jnp.zeros_like(ref)

    for i, row in enumerate(rows):
        ref[i : i + 1, :] += jnp.sum(row, axis=0, keepdims=True)


def row_call(body, name, ids, rows, wholes, outs, sums):
    tokens, width = rows[0].shape
    step = min(128, tokens)
    tile = pl.BlockSpec((step, width), lambda i: (i, 0))
    one = pl.BlockSpec((8, width), lambda i: (0, 0))
    shapes = [jax.ShapeDtypeStruct((tokens, width), t) for t in outs]
    if sums:
        shapes.append(jax.ShapeDtypeStruct((8, width), F32))
    moved = sum(r.size * r.dtype.itemsize for r in rows) + sum(tokens * width * jnp.dtype(t).itemsize for t in outs)
    return pl.pallas_call(
        body,
        grid=(tokens // step,),
        in_specs=[pl.BlockSpec(memory_space=pltpu.SMEM)] + [tile] * len(rows) + [one] * len(wholes),
        out_specs=[tile] * len(outs) + ([one] if sums else []),
        out_shape=shapes,
        compiler_params=pltpu.CompilerParams(vmem_limit_bytes=VMEM_LIMIT),
        cost_estimate=pl.CostEstimate(flops=tokens * width * 10, bytes_accessed=moved, transcendentals=0),
        name=name,
    )(ids, *rows, *wholes)


def rows_first(chips, mixed, ids, hidden):
    def body(ids_ref, x_ref, z_ref):
        z_ref[...] = centre(read_mixed(x_ref, ids_ref, chips, mixed))[0].astype(BF)

    return row_call(body, "rows_first", ids, [hidden], [], [BF], False)[0]


def rows_cot(chips, mixed, ids, cot):
    def body(ids_ref, x_ref, low_ref, sum_ref):
        x = read_mixed(x_ref, ids_ref, chips, mixed)
        low_ref[...] = x.astype(BF)
        add_sums(sum_ref, [x])

    return row_call(body, "rows_cot", ids, [cot], [], [BF], True)


def rows_mid(chips, mixed, ids, hidden, here, swapped, vec):
    def body(ids_ref, x_ref, here_ref, swapped_ref, vec_ref, res_ref, norm_ref):
        added = jnp.where(ids_ref[3] == 1, here_ref[...].astype(F32), swapped_ref[...].astype(F32))
        res = read_mixed(x_ref, ids_ref, chips, mixed) + added + vec_ref[2:3, :]
        res_ref[...] = res
        norm_ref[...] = (centre(res)[0] * vec_ref[3:4, :] + vec_ref[4:5, :]).astype(BF)

    return row_call(body, "rows_mid", ids, [hidden, here, swapped], [vec], [F32, BF], False)


def rows_out(chips, mixed, ids, residual, own, got, vec):
    def body(ids_ref, res_ref, own_ref, got_ref, vec_ref, out_ref):
        out = res_ref[...] + (own_ref[...] + got_ref[...].astype(F32)) + vec_ref[5:6, :]
        write_mixed(out_ref, out, ids_ref, chips, mixed)

    return row_call(body, "rows_out", ids, [residual, own, got], [vec], [F32], False)[0]


def rows_mid_back(chips, mixed, ids, cot, residual, own, got, vec):
    def body(ids_ref, cot_ref, res_ref, own_ref, got_ref, vec_ref, grad_ref, low_ref, sum_ref):
        z, inv = centre(res_ref[...])
        grad = own_ref[...] + got_ref[...].astype(F32)
        mid = read_mixed(cot_ref, ids_ref, chips, mixed) + norm_back(grad, vec_ref[3:4, :], z, inv)
        grad_ref[...] = mid
        low_ref[...] = mid.astype(BF)
        add_sums(sum_ref, [grad * z, grad, mid])

    return row_call(body, "rows_mid_back", ids, [cot, residual, own, got], [vec], [F32, BF], True)


def rows_first_back(chips, mixed, ids, hidden, grad_mid, here, swapped, vec):
    def body(ids_ref, x_ref, mid_ref, here_ref, swapped_ref, vec_ref, out_ref):
        z, inv = centre(read_mixed(x_ref, ids_ref, chips, mixed))
        grad = jnp.where(ids_ref[3] == 1, here_ref[...].astype(F32), swapped_ref[...].astype(F32))
        out = mid_ref[...] + norm_back(grad, vec_ref[0:1, :], z, inv)
        write_mixed(out_ref, out, ids_ref, chips, mixed)

    return row_call(body, "rows_first_back", ids, [hidden, grad_mid, here, swapped], [vec], [F32], False)[0]


class Plan:
    def __init__(self, dp, size, small, d_model, heads, qb, ups, ub):
        self.dp, self.size, self.small, self.d_model = dp, size, small, d_model
        self.heads, self.qb, self.ups, self.ub = heads, qb, ups, ub
        self.chips = dp // 2
        self.pair = heads // 2
        self.n_q = size * 3 * self.pair * HD
        self.n_u = size * (ups // 2) * ub * dp
        self.used = 6 * small + heads * qb + ups * ub

    def vector(self, which, n):
        owner = n // self.small
        t = owner % self.size
        c = (owner // self.size) % 2
        r = owner // (2 * self.size)
        return r, c, t, which * self.small + n % self.small

    def query(self, n, chip, core, tensor):
        per = 3 * self.pair * HD
        part = (n % per) // (self.pair * HD)
        head = (n % (self.pair * HD)) // HD
        b = n % HD + jnp.where(part == 2, HD, 0)
        d = b // self.qb
        place = 6 * self.small + (core * self.pair + head) * self.qb + b % self.qb
        place = jnp.where(part == 1, -1, place)
        return chip ^ (d // 2), d % 2, (tensor + n // per) % self.size, place

    def up(self, n, chip, core, tensor):
        row_len = self.ub * self.dp
        per = (self.ups // 2) * row_len
        row = (n % per) // row_len
        d = (n % row_len) // self.ub
        place = 6 * self.small + self.heads * self.qb + (core * (self.ups // 2) + row) * self.ub + n % self.ub
        return chip ^ (d // 2), d % 2, (tensor + n // per) % self.size, place


def spread_small(plan, ids, table):
    count, pack = table.shape

    def body(ids_ref, table_ref, vec_ref, bq_ref, bu_ref):
        chip, core, tensor = ids_ref[0], ids_ref[1], ids_ref[2]

        def pick(where_, n):
            col = lax.broadcasted_iota(jnp.int32, (1, n), 1)
            r, c, t, place = where_(col)
            hot = lax.broadcasted_iota(jnp.int32, (pack, n), 0) == place
            got = dot_nn(table_ref[...], jnp.where(hot, 1.0, 0.0).astype(BF))
            row = (r * 2 + c) * plan.size + t
            return jnp.sum(
                jnp.where(lax.broadcasted_iota(jnp.int32, (count, n), 0) == row, got, 0.0), axis=0, keepdims=True
            )

        for v in range(6):
            vec_ref[v : v + 1, :] = pick(functools.partial(plan.vector, v), plan.d_model)
        vec_ref[6:8, :] = jnp.zeros((2, plan.d_model), F32)
        bq_ref[...] = pick(lambda n: plan.query(n, chip, core, tensor), plan.n_q)
        bu_ref[...] = pick(lambda n: plan.up(n, chip, core, tensor), plan.n_u)

    return pl.pallas_call(
        body,
        in_specs=[pl.BlockSpec(memory_space=pltpu.SMEM), pl.BlockSpec(memory_space=pltpu.VMEM)],
        out_shape=[
            jax.ShapeDtypeStruct((8, plan.d_model), F32),
            jax.ShapeDtypeStruct((1, plan.n_q), F32),
            jax.ShapeDtypeStruct((1, plan.n_u), F32),
        ],
        compiler_params=pltpu.CompilerParams(vmem_limit_bytes=VMEM_LIMIT),
        cost_estimate=pl.CostEstimate(flops=10**8, bytes_accessed=10**5, transcendentals=0),
        name="spread_small",
    )(ids, table)


def pack_small(plan, ids, mid_sums, cot_sums, bias_q, bias_u):
    size = plan.size
    width = plan.d_model
    per_q, per_u = plan.n_q // size, plan.n_u // size

    def body(ids_ref, mid_ref, cot_ref, bq_ref, bu_ref, out_ref):
        core, tensor = ids_ref[1], ids_ref[2]
        out_ref[...] = jnp.zeros_like(out_ref)
        out_ref[0:2, :] = mid_ref[3:5, :]
        out_ref[2:3, :] = mid_ref[2:3, :]
        out_ref[3:5, :] = mid_ref[0:2, :]
        out_ref[5:6, :] = cot_ref[0:1, :]
        at = 8
        for ref, per in ((bq_ref, per_q), (bu_ref, per_u)):
            x = ref[...]
            turned = x
            for t in range(1, size):
                moved = jnp.concatenate([x[:, (size - t) * per :], x[:, : (size - t) * per]], axis=1)
                turned = jnp.where(tensor == t, moved, turned)
            for c in range(2):
                put = jnp.where(core == c, turned, 0.0)
                for lo in range(0, put.shape[1], width):
                    part = put[:, lo : lo + width]
                    out_ref[at : at + 1, : part.shape[1]] = part
                    at += 1

    lines = 8 + 2 * (-(-plan.n_q // width) - (-plan.n_u // width))
    return pl.pallas_call(
        body,
        in_specs=[pl.BlockSpec(memory_space=pltpu.SMEM)] + [pl.BlockSpec(memory_space=pltpu.VMEM)] * 4,
        out_shape=jax.ShapeDtypeStruct((-(-lines // 8) * 8, width), F32),
        compiler_params=pltpu.CompilerParams(vmem_limit_bytes=VMEM_LIMIT),
        cost_estimate=pl.CostEstimate(flops=10**6, bytes_accessed=10**5, transcendentals=0),
        name="pack_small",
    )(ids, mid_sums, cot_sums, bias_q, bias_u)


def own_small(plan, total, index, tensor):
    size, width = plan.size, plan.d_model
    n_q, n_u = -(-plan.n_q // width), -(-plan.n_u // width)
    vectors = lax.dynamic_slice_in_dim(total[:6], (index % 2 * size + tensor) * plan.small, plan.small, 1)
    q = total[8 : 8 + 2 * n_q].reshape(2, -1)[:, : plan.n_q].reshape(2, size, 3, plan.pair, HD)
    q = lax.dynamic_index_in_dim(q, tensor, 1, keepdims=False)
    q = jnp.stack([q[:, 0], q[:, 2]], axis=2).reshape(plan.heads, 2 * HD)
    q = lax.dynamic_slice_in_dim(q, index * plan.qb, plan.qb, 1)
    u = total[8 + 2 * n_q : 8 + 2 * (n_q + n_u)].reshape(2, -1)[:, : plan.n_u].reshape(2, size, plan.ups // 2, -1)
    u = lax.dynamic_index_in_dim(u, tensor, 1, keepdims=False).reshape(plan.ups, -1)
    u = lax.dynamic_slice_in_dim(u, index * plan.ub, plan.ub, 1)
    return [vectors[i] for i in range(6)], q, u


def qkv_grads(seq_one, grad_qkv, w_qkv, colsum, vec_t):
    seq, d_model = seq_one.shape
    width = grad_qkv.shape[1]
    step = min(256, d_model)

    def body(z_ref, grad_ref, w_ref, col_ref, vec_ref, out_ref, sum_ref):
        g = lax.dot_general(z_ref[...], grad_ref[...], (((0,), (0,)), ((), ())), preferred_element_type=F32)
        w = w_ref[...].astype(F32)
        col = col_ref[...]
        out_ref[...] = (g * vec_ref[:, 0:1] + vec_ref[:, 1:2] * col).astype(BF)
        gain = jnp.sum(g * w, axis=1, keepdims=True)
        shift = jnp.sum(w * col, axis=1, keepdims=True)
        lane = lax.broadcasted_iota(jnp.int32, (step, 128), 1)
        sum_ref[...] = jnp.where(lane == 0, gain, jnp.where(lane == 1, shift, 0.0)).T[:8]

    return pl.pallas_call(
        body,
        grid=(d_model // step,),
        in_specs=[
            pl.BlockSpec((seq, step), lambda i: (0, i)),
            pl.BlockSpec((seq, width), lambda i: (0, 0)),
            pl.BlockSpec((step, width), lambda i: (i, 0)),
            pl.BlockSpec((1, width), lambda i: (0, 0)),
            pl.BlockSpec((step, 128), lambda i: (i, 0)),
        ],
        out_specs=[pl.BlockSpec((step, width), lambda i: (i, 0)), pl.BlockSpec((8, step), lambda i: (0, i))],
        out_shape=[jax.ShapeDtypeStruct((d_model, width), BF), jax.ShapeDtypeStruct((8, d_model), F32)],
        compiler_params=pltpu.CompilerParams(vmem_limit_bytes=VMEM_LIMIT),
        cost_estimate=pl.CostEstimate(
            flops=2 * seq * d_model * width, bytes_accessed=2 * (seq + 2 * d_model) * width, transcendentals=0
        ),
        name="qkv_grads",
    )(seq_one, grad_qkv, w_qkv, colsum, vec_t)


def split_weights(ids, w_qkv, w_out, w_up, w_down):
    rows = w_qkv.shape[0]
    n_q, n_o, n_u = w_qkv.shape[1] // 2, w_out.shape[0] // 2, w_up.shape[1] // 2
    pair = n_q // (3 * HD)
    width = n_q + n_o + 2 * n_u

    def body(ids_ref, q_ref, o_ref, u_ref, d_ref, mine_ref, give_ref):
        core = ids_ref[1]
        for half, ref in ((core, mine_ref), (1 - core, give_ref)):
            x = q_ref[:, pl.ds(pl.multiple_of(half * n_q, n_q), n_q)]
            parts = [
                x[:, (h * 3 + p) * HD : (h * 3 + p + 1) * HD] for p in range(3) for h in range(pair)
            ]
            ref[:, :n_q] = jnp.concatenate(parts, axis=1)
            ref[:, n_q : n_q + n_o] = o_ref[pl.ds(pl.multiple_of(half * n_o, n_o), n_o), :].T
            ref[:, n_q + n_o : n_q + n_o + n_u] = u_ref[:, pl.ds(pl.multiple_of(half * n_u, n_u), n_u)]
            ref[:, n_q + n_o + n_u :] = d_ref[pl.ds(pl.multiple_of(half * n_u, n_u), n_u), :].T

    return pl.pallas_call(
        body,
        in_specs=[pl.BlockSpec(memory_space=pltpu.SMEM)] + [pl.BlockSpec(memory_space=pltpu.VMEM)] * 4,
        out_shape=[jax.ShapeDtypeStruct((rows, width), BF)] * 2,
        compiler_params=pltpu.CompilerParams(vmem_limit_bytes=VMEM_LIMIT),
        cost_estimate=pl.CostEstimate(flops=0, bytes_accessed=rows * width * 8, transcendentals=0),
        name="split_weights",
    )(ids, w_qkv, w_out, w_up, w_down)


def swap_blocks(values, bit, block):
    count = values.shape[1] // block
    return jnp.concatenate([values[:, (r ^ (1 << bit)) * block : ((r ^ (1 << bit)) + 1) * block] for r in range(count)], axis=1)


def local(
    hidden_in,
    ln1_gain,
    ln1_bias,
    qkv_weight,
    qkv_bias,
    out_weight,
    out_bias,
    ln2_gain,
    ln2_bias,
    up_weight,
    up_bias,
    down_weight,
    down_bias,
    cotangent,
):
    dp = lax.axis_size("dp")
    size = lax.axis_size("tensor")
    index = lax.axis_index("dp")
    core = index % 2
    chip = index // 2
    tensor = lax.axis_index("tensor")
    keeps = core == tensor % 2
    chips = dp // 2
    tokens, d_model = hidden_in.shape
    block = d_model // chips
    heads_here = qkv_weight.shape[1] // (3 * HD)
    pair = heads_here // 2
    rows = qkv_weight.shape[0]
    mixed = block % 128 == 0
    ids = jnp.stack([chip, core, tensor, keeps.astype(jnp.int32)]).astype(jnp.int32)
    small = ln1_gain.shape[0]
    plan = Plan(dp, size, small, d_model, heads_here, qkv_bias.shape[1], up_bias.shape[0], up_bias.shape[1])

    def relative(values):
        if mixed:
            return values
        return jnp.concatenate(
            [lax.dynamic_slice_in_dim(values, (chip ^ r) * block, block, 1) for r in range(chips)], axis=1
        )

    wide = [qkv_weight.shape[1] // 2, out_weight.shape[0] // 2, up_weight.shape[1] // 2, down_weight.shape[0] // 2]
    packed = jnp.concatenate(
        [v.reshape(-1) for v in (ln1_gain, ln1_bias, out_bias, ln2_gain, ln2_bias, down_bias, qkv_bias, up_bias)]
    )
    pack = wide[0]
    packed = jnp.pad(packed, (0, pack - packed.shape[0])).reshape(1, pack)
    if mixed:
        own, give = split_weights(ids, qkv_weight, out_weight, up_weight, down_weight)
    else:
        w_q = qkv_weight.reshape(rows, 2, pair, 3, HD).transpose(0, 1, 3, 2, 4).reshape(rows, 2, 3 * pair * HD)
        parts = [w_q] + [w.reshape(rows, 2, -1) for w in (out_weight.T, up_weight, down_weight.T)]
        loc = jnp.concatenate(parts, axis=2).transpose(1, 0, 2)
        own = lax.dynamic_index_in_dim(loc, core, 0, keepdims=False)
        give = lax.dynamic_index_in_dim(loc, 1 - core, 0, keepdims=False)
    other_pack = swap_core(packed)
    piece = both_halves(own, swap_core(give), core)
    slot = jnp.arange(16)[:, None]
    extra = jnp.where(slot == core * size + tensor, packed, jnp.zeros_like(packed))
    extra = jnp.where(slot == (1 - core) * size + tensor, other_pack, extra)

    hidden = relative(hidden_in)
    z_one = rows_first(chips, mixed, ids, hidden)
    seq_one = to_sequence(z_one, core, keeps)
    (w_qkv,), table = gather_weights(piece[:, : wide[0]], wide[:1], extra)
    table = table.reshape(chips, 16, pack)[:, : 2 * size].reshape(chips * 2 * size, pack)
    vec, b_qkv, b_up = spread_small(plan, ids, table)
    (w_out_t, w_up), _ = gather_weights(piece[:, wide[0] : wide[0] + wide[1] + wide[2]], wide[1:3])
    (w_down_t,), _ = gather_weights(piece[:, wide[0] + wide[1] + wide[2] :], wide[3:])
    cot = relative(cotangent)
    cot_low, cot_sums = rows_cot(chips, mixed, ids, cot)
    cot_rows = jnp.concatenate([cot_low, swap_core(cot_low)], axis=0)

    head_ids = ((tensor + jnp.arange(size)) % size)[:, None] * heads_here + core * pair + jnp.arange(pair)[None]
    slopes = jnp.exp2(-8.0 * (head_ids + 1).astype(F32) / H)

    rows_one = (seq_one.astype(F32) * vec[0:1] + vec[1:2]).astype(BF)
    qkv = (dot_nn(rows_one, w_qkv) + b_qkv).astype(BF)
    context, lse = attend(qkv, slopes)
    here, swapped = from_sequence(context, w_out_t, core)
    residual, norm_two = rows_mid(chips, mixed, ids, hidden, here, swapped, vec)

    rows_two = jnp.concatenate([norm_two, swap_core(norm_two)], axis=0)
    up_pre = dot_nn(rows_two, w_up) + b_up
    active = gelu_tanh(up_pre).astype(BF)
    got_down = swap_core(dot_nt(active[tokens:], w_down_t).astype(BF))
    own_down = dot_nt(active[:tokens], w_down_t)
    output = rows_out(chips, mixed, ids, residual, own_down, got_down, vec)

    grad_active = dot_nn(cot_rows, w_down_t)
    _, gelu_back = jax.vjp(gelu_tanh, up_pre)
    grad_pre = gelu_back(grad_active)[0].astype(BF)
    got_two = swap_core(dot_nt(grad_pre[tokens:], w_up).astype(BF))
    own_two = dot_nt(grad_pre[:tokens], w_up)
    g_down_t = dot_tn(cot_rows, active).astype(BF)
    sum_down = scatter_grads(g_down_t, core)
    g_up = dot_tn(rows_two, grad_pre).astype(BF)
    sum_up = scatter_grads(g_up, core)
    grad_b_up = jnp.sum(grad_pre.astype(F32), axis=0, keepdims=True)
    grad_mid, mid_low, mid_sums = rows_mid_back(chips, mixed, ids, cot, residual, own_two, got_two, vec)

    mid_rows = to_sequence(mid_low, core, keeps)
    grad_context = dot_nn(mid_rows, w_out_t).astype(BF)
    g_out_t = dot_tn(mid_rows, context).astype(BF)
    grad_qkv, grad_b_qkv = attend_back(qkv, slopes, lse, grad_context)
    grad_b_qkv = grad_b_qkv.reshape(1, -1)
    vec_t = jnp.pad(vec[:8].T, ((0, 0), (0, 120)))
    g_qkv, one_sums = qkv_grads(seq_one, grad_qkv, w_qkv, grad_b_qkv, vec_t)
    sum_out = scatter_grads(g_out_t, core)
    sum_qkv = scatter_grads(g_qkv, core)
    here, swapped = from_sequence(grad_qkv, w_qkv, core)
    grad_in = rows_first_back(chips, mixed, ids, hidden, grad_mid, here, swapped, vec)

    mid_sums = jnp.concatenate([mid_sums[:3], one_sums[:2], mid_sums[5:]], axis=0)
    total = pack_small(plan, ids, mid_sums, cot_sums, grad_b_qkv, grad_b_up)
    total = total + swap_core(total)
    for bit in range(chip_bits()):
        got = swap_bit(total, bit + 1)
        total = total + jnp.concatenate([swap_blocks(got[:8], bit, block), got[8:]], axis=0)
    for bit in range((size - 1).bit_length()):
        total = total + lax.ppermute(total, "tensor", [(i, i ^ (1 << bit)) for i in range(size)])
    vector_sums, sum_b_qkv, sum_b_up = own_small(plan, total, index, tensor)

    sum_w_qkv = sum_qkv.reshape(rows, 2, 3, pair, HD).transpose(0, 1, 3, 2, 4).reshape(rows, -1)
    return (
        relative(output),
        relative(grad_in),
        vector_sums[0],
        vector_sums[1],
        sum_w_qkv,
        sum_b_qkv,
        sum_out.reshape(rows, -1).T,
        vector_sums[2],
        vector_sums[3],
        vector_sums[4],
        sum_up.reshape(rows, -1),
        sum_b_up,
        sum_down.reshape(rows, -1).T,
        vector_sums[5],
    )


def solution(mesh):
    both = P(("dp", "tensor"))
    wide = P(("dp", "tensor"), None)
    split, turned = P("dp", "tensor"), P("tensor", "dp")
    return jax.shard_map(
        local,
        mesh=mesh,
        in_specs=(wide, both, both, split, turned, turned, both, both, both, split, turned, turned, both, wide),
        out_specs=(wide, wide, both, both, split, turned, turned, both, both, both, split, turned, turned, both),
        check_vma=False,
    )
```

```python
import functools

import jax
import jax.numpy as jnp
from jax import lax
from jax.experimental import pallas as pl
from jax.experimental.pallas import tpu as pltpu
from jax.sharding import PartitionSpec as P

H = 16
HD = 64
FF = 4096
SEQ_LEN = 1024
EPSILON = 1e-05
MASKED = -1e30
BF = jnp.bfloat16
F32 = jnp.float32


def gelu_tanh(values):
    inner = 0.7978845608028654 * (values + 0.044715 * values * values * values)
    return 0.5 * values * (1.0 + jnp.tanh(inner))


def dot_nn(left, right):
    return lax.dot_general(left, right, (((1,), (0,)), ((), ())), preferred_element_type=F32)


def dot_tn(left, right):
    return lax.dot_general(left, right, (((0,), (0,)), ((), ())), preferred_element_type=F32)


def dot_nt(left, right):
    return lax.dot_general(left, right, (((1,), (1,)), ((), ())), preferred_element_type=F32)


def swap_bit(values, bit):
    size = lax.axis_size("dp")
    return lax.ppermute(values, "dp", [(i, i ^ (1 << bit)) for i in range(size)])


def swap_core(values):
    return swap_bit(values, 0)


def from_tensor(values, step):
    size = lax.axis_size("tensor")
    return lax.ppermute(values, "tensor", [(i, (i - step) % size) for i in range(size)])


def swap_pair(values):
    dp, tensor = lax.axis_size("dp"), lax.axis_size("tensor")
    pairs = []
    for d in range(dp):
        for t in range(tensor):
            if d % 2 != t % 2:
                pairs.append((d * tensor + t, (d ^ 1) * tensor + (t ^ 1)))
    return lax.ppermute(values, ("dp", "tensor"), pairs)


def chip_bits():
    return (lax.axis_size("dp") // 2).bit_length() - 1


def tie(*values):
    return lax.optimization_barrier(values)


def gather_line(piece, widths, turned, extra_rows=0):
    rows = piece.shape[0] - extra_rows
    turned = [piece] + list(turned)
    cols, at = [], 0
    for width in widths:
        cols += [t[:rows, at : at + width] for t in turned]
        at += width
    line = jnp.concatenate(cols, axis=1)
    if extra_rows:
        added = functools.reduce(jnp.add, [t[rows:] for t in turned])
        added = jnp.pad(added, ((0, 0), (0, line.shape[1] - added.shape[1])))
        line = jnp.concatenate([line, added], axis=0)
    return line


def exchange(*moves):
    values = lax.optimization_barrier(tuple(v for _, v in moves))
    return lax.optimization_barrier(tuple(move(v) for (move, _), v in zip(moves, values)))


def by_bit(bit):
    return functools.partial(swap_bit, bit=bit)


def by_tensor(step):
    return functools.partial(from_tensor, step=step)


def along_tensor(piece):
    return [(by_tensor(k), piece) for k in range(1, lax.axis_size("tensor"))]


def gather_near(line):
    return [(by_bit(1), line), (by_bit(2), line)] if chip_bits() == 2 else []


def gather_far(near, split):
    return [(by_bit(2), near[0][:split]), (by_bit(1), near[1][split:])] if chip_bits() == 2 else []


def gathered(line, near, far, split):
    if chip_bits() == 2:
        return [[v[:split], v[split:]] for v in (line, *near)] + [list(far)]
    held = line[None]
    for bit in range(chip_bits()):
        held = jnp.concatenate([held, swap_bit(held, bit + 1)], axis=0)
    return [[held[r, :split], held[r, split:]] for r in range(held.shape[0])]


def join_chips(got, widths, rows):
    size = lax.axis_size("tensor")
    out, at = [], 0
    for width in widths:
        cut = slice(at, at + size * width)
        out.append(jnp.concatenate([part for top, low in got for part in (top[:, cut], low[: rows - rows // 2, cut])]))
        at += size * width
    return out


def take(grads, low, high):
    return jnp.concatenate([g[low:high] for g in grads], axis=1) if len(grads) > 1 else grads[0][low:high]


def low_half(rows, r, grads, extra):
    low = take(grads, r * rows + rows // 2, (r + 1) * rows)
    return low if extra is None else jnp.concatenate([low, extra[r * 16 : (r + 1) * 16]], axis=0)


def scatter_far(rows, *grads, extra=None):
    if chip_bits() != 2:
        return []
    return [(by_bit(2), take(grads, 3 * rows, 3 * rows + rows // 2)), (by_bit(1), low_half(rows, 3, grads, extra))]


def scatter_near(rows, far, *grads, extra=None):
    if chip_bits() != 2:
        return []
    split = rows // 2
    top = (take(grads, rows, rows + split).astype(F32) + far[0].astype(F32)).astype(BF)
    low = (low_half(rows, 2, grads, extra).astype(F32) + far[1].astype(F32)).astype(BF)
    return [
        (by_bit(1), jnp.concatenate([top, low_half(rows, 1, grads, extra)], axis=0)),
        (by_bit(2), jnp.concatenate([take(grads, 2 * rows, 2 * rows + split), low], axis=0)),
    ]


def scattered(rows, near, *grads, extra=None):
    if chip_bits() == 2:
        own = jnp.concatenate([take(grads, 0, rows // 2), low_half(rows, 0, grads, extra)], axis=0)
        return own.astype(F32) + near[0].astype(F32) + near[1].astype(F32)
    grad = take(grads, 0, grads[0].shape[0])
    held = grad.reshape(-1, rows, grad.shape[1])
    for bit in range(chip_bits())[::-1]:
        half = held.shape[0] // 2
        got = swap_bit(held[half:], bit + 1)
        held = (held[:half].astype(F32) + got.astype(F32)).astype(BF)
    return held[0].astype(F32)


def scatter_tensor(blocks):
    size = lax.axis_size("tensor")
    return [(by_tensor(size - k), blocks[k].astype(BF)) for k in range(1, size)]


def cut_blocks(line):
    size = lax.axis_size("tensor")
    width = line.shape[1] // size
    return [line[:, k * width : (k + 1) * width] for k in range(size)]


def scatter_total(blocks, got):
    return functools.reduce(jnp.add, [part.astype(F32) for part in (blocks[0], *got)])


def core_rows(values, core):
    half = values.shape[0] // 2
    keep = lax.dynamic_slice_in_dim(values, core * half, half, 0)
    return keep, lax.dynamic_slice_in_dim(values, (1 - core) * half, half, 0)


def by_core(keep, back, core):
    return jnp.where(core == 0, jnp.stack([keep, back], 1), jnp.stack([back, keep], 1))


def both_halves(mine, other, core):
    return jnp.concatenate([jnp.where(core == 0, mine, other), jnp.where(core == 0, other, mine)], axis=0)


BLOCK_Q = 256


def cost(microseconds):
    return pl.CostEstimate(flops=int(microseconds * 1.1e9), bytes_accessed=int(microseconds * 1e6), transcendentals=0)


def biased_pair(q, k, slope_ref, group, head):
    seq = k.shape[0]
    lane = lax.broadcasted_iota(jnp.int32, (1, 2 * HD), 1)
    mine = (lane >= head * HD) & (lane < (head + 1) * HD)
    slot = lane & (HD - 1)
    bias = slope_ref[group, head] * lax.broadcasted_iota(jnp.int32, (seq, 2 * HD), 0).astype(F32)
    high = bias.astype(BF)
    rest = bias - high.astype(F32)
    middle = rest.astype(BF)
    low = (rest - middle.astype(F32)).astype(BF)
    zero = jnp.zeros_like(k)
    extra = jnp.where(slot == 0, high, jnp.where(slot == 1, middle, jnp.where(slot == 2, low, zero)))
    ones = jnp.where(slot < 3, 1.0, 0.0).astype(BF)
    return jnp.where(mine, q, jnp.broadcast_to(ones, q.shape)), jnp.where(mine, k, extra), mine


def below_diagonal(size):
    keys = lax.broadcasted_iota(jnp.int32, (size, size), 0)
    return keys <= lax.broadcasted_iota(jnp.int32, (size, size), 1)


def attend_kernel(start, slope_ref, qkv_ref, *refs):
    ctx_ref, lse_ref = refs[-2:]
    group = pl.program_id(0) + start
    wide = 2 * HD
    seq = qkv_ref.shape[0]
    size = min(BLOCK_Q, seq)
    q = qkv_ref[:, :wide] * BF(HD**-0.5)
    k = qkv_ref[:, wide : 2 * wide]
    v_t = qkv_ref[:, 2 * wide :].T
    heads = [biased_pair(q, k, slope_ref, group, h) for h in range(2)]
    seen = below_diagonal(size)
    for i in range(seq // size):
        lo, hi = i * size, (i + 1) * size
        outs = []
        for h, (qh, kh, _) in enumerate(heads):
            s = dot_nt(kh[:hi], qh[lo:hi])
            last = jnp.where(seen, s[lo:], MASKED)
            top = jnp.max(last, axis=0, keepdims=True)
            if i:
                top = jnp.maximum(top, jnp.max(s[:lo], axis=0, keepdims=True))
            e = jnp.exp(last - top)
            total = jnp.sum(e, axis=0, keepdims=True)
            e = e.astype(BF)
            if i:
                e0 = jnp.exp(s[:lo] - top)
                total = total + jnp.sum(e0, axis=0, keepdims=True)
                e = jnp.concatenate([e0.astype(BF), e], axis=0)
            o_t = dot_nn(v_t[h * HD : (h + 1) * HD, :hi], e)
            outs.append(o_t * (1.0 / total))
            lse_ref[0, h : h + 1, lo:hi] = top + jnp.log(total)
        ctx_ref[lo:hi, :] = jnp.concatenate(outs, axis=0).T.astype(BF)


def attend(qkv, slopes, first, groups, *earlier):
    seq = qkv.shape[0]
    wide = 2 * HD
    return pl.pallas_call(
        functools.partial(attend_kernel, first),
        grid=(groups,),
        in_specs=[
            pl.BlockSpec(memory_space=pltpu.SMEM),
            pl.BlockSpec((seq, 3 * wide), lambda g: (0, g + first)),
        ]
        + [pl.BlockSpec(memory_space=pl.ANY)] * len(earlier),
        out_specs=[
            pl.BlockSpec((seq, wide), lambda g: (0, g)),
            pl.BlockSpec((1, 2, seq), lambda g: (g, 0, 0)),
        ],
        out_shape=[
            jax.ShapeDtypeStruct((seq, groups * wide), BF),
            jax.ShapeDtypeStruct((groups, 2, seq), F32),
        ],
        compiler_params=pltpu.CompilerParams(vmem_limit_bytes=48 * 1024 * 1024),
        cost_estimate=cost(9),
        name="attend",
    )(slopes, qkv, *earlier)


def attend_back_kernel(start, slope_ref, qkv_ref, grad_ref, lse_ref, *refs):
    out_ref, bias_ref, dk_ref, dv_ref = refs[-4:]
    group = pl.program_id(0) + start
    wide = 2 * HD
    seq = qkv_ref.shape[0]
    size = min(BLOCK_Q, seq)
    q = qkv_ref[:, :wide] * BF(HD**-0.5)
    k = qkv_ref[:, wide : 2 * wide]
    v = qkv_ref[:, 2 * wide :]
    k_t = k.T
    zero = jnp.zeros_like(q)
    heads = [biased_pair(q, k, slope_ref, group, h) for h in range(2)]
    clean = [jnp.where(mine, q, zero) for _, _, mine in heads]
    grads = [jnp.where(mine, grad_ref[...], zero) for _, _, mine in heads]
    seen = below_diagonal(size)
    dk_ref[...] = jnp.zeros_like(dk_ref)
    dv_ref[...] = jnp.zeros_like(dv_ref)
    bias_q = jnp.zeros((1, wide), F32)
    for i in range(seq // size):
        lo, hi = i * size, (i + 1) * size
        outs = []
        for h, (qh, kh, _) in enumerate(heads):
            s = dot_nt(kh[:hi], qh[lo:hi])
            lse = lse_ref[0, h : h + 1, lo:hi]
            p = jnp.exp(jnp.where(seen, s[lo:], MASKED) - lse)
            if i:
                p = jnp.concatenate([jnp.exp(s[:lo] - lse), p], axis=0)
            dp = dot_nt(v[:hi], grads[h][lo:hi])
            inner = jnp.sum(p * dp, axis=0, keepdims=True)
            ds = (p * (dp - inner)).astype(BF)
            dk_ref[:hi, :] += dot_nn(ds, clean[h][lo:hi])
            dv_ref[:hi, :] += dot_nn(p.astype(BF), grads[h][lo:hi])
            outs.append(dot_nn(k_t[h * HD : (h + 1) * HD, :hi], ds))
        dq = (jnp.concatenate(outs, axis=0).T * HD**-0.5).astype(BF)
        bias_q = bias_q + jnp.sum(dq.astype(F32), axis=0, keepdims=True)
        out_ref[lo:hi, :wide] = dq
    dk = dk_ref[...].astype(BF)
    out_ref[:, wide : 2 * wide] = dk
    dv = dv_ref[...].astype(BF)
    out_ref[:, 2 * wide :] = dv
    bias_ref[0, :, :wide] = bias_q
    bias_ref[0, :, wide : 2 * wide] = jnp.sum(dk.astype(F32), axis=0, keepdims=True)
    bias_ref[0, :, 2 * wide :] = jnp.sum(dv.astype(F32), axis=0, keepdims=True)


def attend_back(qkv, slopes, lse, grad_ctx, first, groups, *earlier):
    seq = qkv.shape[0]
    wide = 2 * HD
    return pl.pallas_call(
        functools.partial(attend_back_kernel, first),
        grid=(groups,),
        in_specs=[
            pl.BlockSpec(memory_space=pltpu.SMEM),
            pl.BlockSpec((seq, 3 * wide), lambda g: (0, g + first)),
            pl.BlockSpec((seq, wide), lambda g: (0, g + first)),
            pl.BlockSpec((1, 2, seq), lambda g: (g, 0, 0)),
        ]
        + [pl.BlockSpec(memory_space=pl.ANY)] * len(earlier),
        out_specs=[
            pl.BlockSpec((seq, 3 * wide), lambda g: (0, g)),
            pl.BlockSpec((1, 1, 3 * wide), lambda g: (g, 0, 0)),
        ],
        out_shape=[
            jax.ShapeDtypeStruct((seq, groups * 3 * wide), BF),
            jax.ShapeDtypeStruct((groups, 1, 3 * wide), F32),
        ],
        scratch_shapes=[pltpu.VMEM((seq, wide), F32), pltpu.VMEM((seq, wide), F32)],
        compiler_params=pltpu.CompilerParams(vmem_limit_bytes=48 * 1024 * 1024),
        cost_estimate=cost(11),
        name="attend_back",
    )(slopes, qkv, grad_ctx, lse, *earlier)


VMEM_LIMIT = 48 * 1024 * 1024


def read_mixed(ref, ids_ref, chips, mixed):
    if not mixed:
        return ref[...]
    block = ref.shape[1] // chips
    parts = [ref[:, pl.ds(pl.multiple_of((ids_ref[0] ^ r) * block, block), block)] for r in range(chips)]
    return jnp.concatenate(parts, axis=1)


def write_mixed(ref, values, ids_ref, chips, mixed):
    if not mixed:
        ref[...] = values
        return
    block = ref.shape[1] // chips
    for r in range(chips):
        ref[:, pl.ds(pl.multiple_of((ids_ref[0] ^ r) * block, block), block)] = values[:, r * block : (r + 1) * block]


def centre(x):
    mean_row = jnp.mean(x, axis=1, keepdims=True)
    centred = x - mean_row
    inv = lax.rsqrt(jnp.mean(centred * centred, axis=1, keepdims=True) + EPSILON)
    return centred * inv, inv


def norm_back(grad, gain, z, inv):
    g = grad * gain
    mean_g = jnp.mean(g, axis=1, keepdims=True)
    mean_gz = jnp.mean(g * z, axis=1, keepdims=True)
    return inv * (g - mean_g - z * mean_gz)


def add_sums(ref, rows):
    @pl.when(pl.program_id(0) == 0)
    def _():
        ref[...] = jnp.zeros_like(ref)

    for i, row in enumerate(rows):
        ref[i : i + 1, :] += jnp.sum(row, axis=0, keepdims=True)


def row_call(body, name, ids, rows, wholes, outs, sums):
    tokens, width = rows[0].shape
    step = min(128, tokens)
    tile = pl.BlockSpec((step, width), lambda i: (i, 0))
    one = pl.BlockSpec((8, width), lambda i: (0, 0))
    shapes = [jax.ShapeDtypeStruct((tokens, width), t) for t in outs]
    if sums:
        shapes.append(jax.ShapeDtypeStruct((8, width), F32))
    moved = sum(r.size * r.dtype.itemsize for r in rows) + sum(tokens * width * jnp.dtype(t).itemsize for t in outs)
    return pl.pallas_call(
        body,
        grid=(tokens // step,),
        in_specs=[pl.BlockSpec(memory_space=pltpu.SMEM)] + [tile] * len(rows) + [one] * len(wholes),
        out_specs=[tile] * len(outs) + ([one] if sums else []),
        out_shape=shapes,
        compiler_params=pltpu.CompilerParams(vmem_limit_bytes=VMEM_LIMIT),
        cost_estimate=cost(3),
        name=name,
    )(ids, *rows, *wholes)


def chosen(own, swapped_ref, ids_ref):
    return jnp.where(ids_ref[3] == 1, own, swapped_ref[...].astype(F32))


def rows_low(chips, mixed, ids, values, sums):
    def body(ids_ref, x_ref, low_ref, *sum_refs):
        x = read_mixed(x_ref, ids_ref, chips, mixed)
        low_ref[...] = x.astype(BF)
        if sums:
            add_sums(sum_refs[0], [x])

    return row_call(body, "rows_low", ids, [values], [], [BF], sums)


def rows_first(chips, mixed, ids, hidden, swapped):
    def body(ids_ref, x_ref, swapped_ref, here_ref, z_ref):
        x = chosen(read_mixed(x_ref, ids_ref, chips, mixed), swapped_ref, ids_ref)
        here_ref[...] = x
        z_ref[...] = centre(x)[0].astype(BF)

    return row_call(body, "rows_first", ids, [hidden, swapped], [], [F32, BF], False)


def rows_mid(ids, hidden, added, vec):
    def body(ids_ref, x_ref, added_ref, vec_ref, res_ref, norm_ref):
        res = x_ref[...] + added_ref[...].astype(F32) + vec_ref[2:3, :]
        res_ref[...] = res
        norm_ref[...] = (centre(res)[0] * vec_ref[3:4, :] + vec_ref[4:5, :]).astype(BF)

    return row_call(body, "rows_mid", ids, [hidden, added], [vec], [F32, BF], False)


def rows_out(ids, residual, own, got, vec):
    def body(ids_ref, res_ref, own_ref, got_ref, vec_ref, out_ref, low_ref):
        out = res_ref[...] + (own_ref[...] + got_ref[...].astype(F32)) + vec_ref[5:6, :]
        out_ref[...] = out
        low_ref[...] = out.astype(BF)

    return row_call(body, "rows_out", ids, [residual, own, got], [vec], [F32, BF], False)


def rows_mid_back(chips, mixed, ids, cot, swapped, residual, own, got, vec):
    def body(ids_ref, cot_ref, swapped_ref, res_ref, own_ref, got_ref, vec_ref, grad_ref, low_ref, sum_ref):
        z, inv = centre(res_ref[...])
        grad = own_ref[...] + got_ref[...].astype(F32)
        above = chosen(read_mixed(cot_ref, ids_ref, chips, mixed), swapped_ref, ids_ref)
        mid = above + norm_back(grad, vec_ref[3:4, :], z, inv)
        grad_ref[...] = mid
        low_ref[...] = mid.astype(BF)
        add_sums(sum_ref, [grad * z, grad, mid])

    return row_call(body, "rows_mid_back", ids, [cot, swapped, residual, own, got], [vec], [F32, BF], True)


def rows_first_back(ids, hidden, grad_mid, own, got, vec):
    def body(ids_ref, x_ref, mid_ref, own_ref, got_ref, vec_ref, out_ref, low_ref):
        z, inv = centre(x_ref[...])
        out = mid_ref[...] + norm_back(own_ref[...] + got_ref[...].astype(F32), vec_ref[0:1, :], z, inv)
        out_ref[...] = out
        low_ref[...] = out.astype(BF)

    return row_call(body, "rows_first_back", ids, [hidden, grad_mid, own, got], [vec], [F32, BF], False)


def rows_home(chips, mixed, ids, here, swapped):
    def body(ids_ref, here_ref, swapped_ref, out_ref):
        write_mixed(out_ref, chosen(here_ref[...], swapped_ref, ids_ref), ids_ref, chips, mixed)

    return row_call(body, "rows_home", ids, [here, swapped], [], [F32], False)[0]


class Plan:
    def __init__(self, dp, size, small, d_model, heads, qb, ups, ub):
        self.dp, self.size, self.small, self.d_model = dp, size, small, d_model
        self.heads, self.qb, self.ups, self.ub = heads, qb, ups, ub
        self.chips = dp // 2
        self.pair = heads // 2
        self.n_q = size * 3 * self.pair * HD
        self.n_u = size * (ups // 2) * ub * dp
        self.used = 6 * small + heads * qb + ups * ub

    def vector(self, which, n):
        owner = n // self.small
        t = owner % self.size
        c = (owner // self.size) % 2
        r = owner // (2 * self.size)
        return r, c, t, which * self.small + n % self.small

    def query(self, n, chip, core, tensor):
        per = 3 * self.pair * HD
        part = (n % per) // (self.pair * HD)
        head = (n % (self.pair * HD)) // HD
        b = n % HD + jnp.where(part == 2, HD, 0)
        d = b // self.qb
        place = 6 * self.small + (core * self.pair + head) * self.qb + b % self.qb
        place = jnp.where(part == 1, -1, place)
        return chip ^ (d // 2), d % 2, (tensor + n // per) % self.size, place

    def up(self, n, chip, core, tensor):
        row_len = self.ub * self.dp
        per = (self.ups // 2) * row_len
        row = (n % per) // row_len
        d = (n % row_len) // self.ub
        place = 6 * self.small + self.heads * self.qb + (core * (self.ups // 2) + row) * self.ub + n % self.ub
        return chip ^ (d // 2), d % 2, (tensor + n // per) % self.size, place


def spread_small(plan, ids, table):
    count, pack = table.shape

    def body(ids_ref, table_ref, vec_ref, bq_ref, bu_ref):
        chip, core, tensor = ids_ref[0], ids_ref[1], ids_ref[2]

        def pick(where_, n):
            col = lax.broadcasted_iota(jnp.int32, (1, n), 1)
            r, c, t, place = where_(col)
            hot = lax.broadcasted_iota(jnp.int32, (pack, n), 0) == place
            got = dot_nn(table_ref[...], jnp.where(hot, 1.0, 0.0).astype(BF))
            row = (r * 2 + c) * plan.size + t
            return jnp.sum(
                jnp.where(lax.broadcasted_iota(jnp.int32, (count, n), 0) == row, got, 0.0), axis=0, keepdims=True
            )

        for v in range(6):
            vec_ref[v : v + 1, :] = pick(functools.partial(plan.vector, v), plan.d_model)
        vec_ref[6:8, :] = jnp.zeros((2, plan.d_model), F32)
        bq_ref[...] = pick(lambda n: plan.query(n, chip, core, tensor), plan.n_q)
        bu_ref[...] = pick(lambda n: plan.up(n, chip, core, tensor), plan.n_u)

    return pl.pallas_call(
        body,
        in_specs=[pl.BlockSpec(memory_space=pltpu.SMEM), pl.BlockSpec(memory_space=pltpu.VMEM)],
        out_shape=[
            jax.ShapeDtypeStruct((8, plan.d_model), F32),
            jax.ShapeDtypeStruct((1, plan.n_q), F32),
            jax.ShapeDtypeStruct((1, plan.n_u), F32),
        ],
        compiler_params=pltpu.CompilerParams(vmem_limit_bytes=VMEM_LIMIT),
        cost_estimate=cost(2),
        name="spread_small",
    )(ids, table)


def pack_small(plan, ids, mid_sums, cot_sums, bias_q, bias_u):
    size = plan.size
    width = plan.d_model
    per_q, per_u = plan.n_q // size, plan.n_u // size

    def body(ids_ref, mid_ref, cot_ref, bq_ref, bu_ref, out_ref):
        core, tensor = ids_ref[1], ids_ref[2]
        out_ref[...] = jnp.zeros_like(out_ref)
        out_ref[0:2, :] = mid_ref[3:5, :]
        out_ref[2:3, :] = mid_ref[2:3, :]
        out_ref[3:5, :] = mid_ref[0:2, :]
        out_ref[5:6, :] = cot_ref[0:1, :]
        at = 8
        for ref, per in ((bq_ref, per_q), (bu_ref, per_u)):
            x = ref[...]
            turned = x
            for t in range(1, size):
                moved = jnp.concatenate([x[:, (size - t) * per :], x[:, : (size - t) * per]], axis=1)
                turned = jnp.where(tensor == t, moved, turned)
            for c in range(2):
                put = jnp.where(core == c, turned, 0.0)
                for lo in range(0, put.shape[1], width):
                    part = put[:, lo : lo + width]
                    out_ref[at : at + 1, : part.shape[1]] = part
                    at += 1

    lines = 8 + 2 * (-(-plan.n_q // width) - (-plan.n_u // width))
    return pl.pallas_call(
        body,
        in_specs=[pl.BlockSpec(memory_space=pltpu.SMEM)] + [pl.BlockSpec(memory_space=pltpu.VMEM)] * 4,
        out_shape=jax.ShapeDtypeStruct((-(-lines // 8) * 8, width), F32),
        compiler_params=pltpu.CompilerParams(vmem_limit_bytes=VMEM_LIMIT),
        cost_estimate=cost(1),
        name="pack_small",
    )(ids, mid_sums, cot_sums, bias_q, bias_u)


def pack_rows(plan, ids, width, mid_sums, cot_sums, bias_q, bias_u):
    size, chips = plan.size, plan.chips

    def body(ids_ref, mid_ref, cot_ref, bq_ref, bu_ref, out_ref):
        chip, core, tensor = ids_ref[0], ids_ref[1], ids_ref[2]

        def put(where_, values):
            n = values.shape[1]
            r, c, t, place = where_(lax.broadcasted_iota(jnp.int32, (1, n), 1))
            hot = lax.broadcasted_iota(jnp.int32, (width, n), 0) == place
            row = (r * 2 + c) * size + (t - tensor + size) % size
            at = lax.broadcasted_iota(jnp.int32, (chips * 2 * size, n), 0) == row
            return dot_nt(jnp.where(at, values, 0.0).astype(BF), jnp.where(hot, 1.0, 0.0).astype(BF))

        rows = [mid_ref[3:4, :], mid_ref[4:5, :], mid_ref[2:3, :], mid_ref[0:1, :], mid_ref[1:2, :], cot_ref[0:1, :]]
        total = put(lambda n: plan.query(n, chip, core, tensor), bq_ref[...])
        total = total + put(lambda n: plan.up(n, chip, core, tensor), bu_ref[...])
        for v, row in enumerate(rows):
            total = total + put(functools.partial(plan.vector, v), row)
        for r in range(chips):
            lines = [
                jnp.concatenate([total[(r * 2 + c) * size + k :][:1] for k in range(size)], axis=1) for c in range(2)
            ]
            lines.append(jnp.zeros((14, size * width), F32))
            out_ref[r * 16 : (r + 1) * 16, :] = jnp.concatenate(lines, axis=0).astype(BF)

    return pl.pallas_call(
        body,
        in_specs=[pl.BlockSpec(memory_space=pltpu.SMEM)] + [pl.BlockSpec(memory_space=pltpu.VMEM)] * 4,
        out_shape=jax.ShapeDtypeStruct((chips * 16, size * width), BF),
        compiler_params=pltpu.CompilerParams(vmem_limit_bytes=VMEM_LIMIT),
        cost_estimate=cost(2),
        name="pack_rows",
    )(ids, mid_sums, cot_sums, bias_q, bias_u)


def own_small(plan, total, index, tensor):
    size, width = plan.size, plan.d_model
    n_q, n_u = -(-plan.n_q // width), -(-plan.n_u // width)
    vectors = lax.dynamic_slice_in_dim(total[:6], (index % 2 * size + tensor) * plan.small, plan.small, 1)
    q = total[8 : 8 + 2 * n_q].reshape(2, -1)[:, : plan.n_q].reshape(2, size, 3, plan.pair, HD)
    q = lax.dynamic_index_in_dim(q, tensor, 1, keepdims=False)
    q = jnp.stack([q[:, 0], q[:, 2]], axis=2).reshape(plan.heads, 2 * HD)
    q = lax.dynamic_slice_in_dim(q, index * plan.qb, plan.qb, 1)
    u = total[8 + 2 * n_q : 8 + 2 * (n_q + n_u)].reshape(2, -1)[:, : plan.n_u].reshape(2, size, plan.ups // 2, -1)
    u = lax.dynamic_index_in_dim(u, tensor, 1, keepdims=False).reshape(plan.ups, -1)
    u = lax.dynamic_slice_in_dim(u, index * plan.ub, plan.ub, 1)
    return [vectors[i] for i in range(6)], q, u


def qkv_grads(seq_one, grad_qkv, w_qkv, part, colsum, vec_t, *earlier):
    seq, d_model = seq_one.shape
    width = grad_qkv.shape[1]
    step = min(256, d_model)

    def body(z_ref, grad_ref, w_ref, col_ref, vec_ref, *refs):
        out_ref, sum_ref = refs[-2:]
        g = lax.dot_general(z_ref[...], grad_ref[...], (((0,), (0,)), ((), ())), preferred_element_type=F32)
        w = w_ref[...].astype(F32)
        col = col_ref[...]
        out_ref[...] = (g * vec_ref[:, 0:1] + vec_ref[:, 1:2] * col).astype(BF)
        gain = jnp.sum(g * w, axis=1, keepdims=True)
        shift = jnp.sum(w * col, axis=1, keepdims=True)
        lane = lax.broadcasted_iota(jnp.int32, (step, 128), 1)
        sum_ref[...] = jnp.where(lane == 0, gain, jnp.where(lane == 1, shift, 0.0)).T[:8]

    return pl.pallas_call(
        body,
        grid=(d_model // step,),
        in_specs=[
            pl.BlockSpec((seq, step), lambda i: (0, i)),
            pl.BlockSpec((seq, width), lambda i: (0, 0)),
            pl.BlockSpec((step, width), lambda i: (i, part)),
            pl.BlockSpec((1, width), lambda i: (0, 0)),
            pl.BlockSpec((step, 128), lambda i: (i, 0)),
        ]
        + [pl.BlockSpec(memory_space=pl.ANY)] * len(earlier),
        out_specs=[pl.BlockSpec((step, width), lambda i: (i, 0)), pl.BlockSpec((8, step), lambda i: (0, i))],
        out_shape=[jax.ShapeDtypeStruct((d_model, width), BF), jax.ShapeDtypeStruct((8, d_model), F32)],
        compiler_params=pltpu.CompilerParams(vmem_limit_bytes=VMEM_LIMIT),
        cost_estimate=cost(5),
        name="qkv_grads",
    )(seq_one, grad_qkv, w_qkv, colsum, vec_t, *earlier)


def split_weights(ids, w_qkv, w_out, w_up, w_down):
    rows = w_qkv.shape[0]
    n_q, n_o, n_u = w_qkv.shape[1] // 2, w_out.shape[0] // 2, w_up.shape[1] // 2
    pair = n_q // (3 * HD)
    width = n_q + n_o + 2 * n_u

    def body(ids_ref, q_ref, o_ref, u_ref, d_ref, mine_ref, give_ref):
        core = ids_ref[1]
        for half, ref in ((core, mine_ref), (1 - core, give_ref)):
            x = q_ref[:, pl.ds(pl.multiple_of(half * n_q, n_q), n_q)]
            parts = [
                x[:, (h * 3 + p) * HD : (h * 3 + p + 1) * HD] for p in range(3) for h in range(pair)
            ]
            ref[:, :n_q] = jnp.concatenate(parts, axis=1)
            ref[:, n_q : n_q + n_o] = o_ref[pl.ds(pl.multiple_of(half * n_o, n_o), n_o), :].T
            ref[:, n_q + n_o : n_q + n_o + n_u] = u_ref[:, pl.ds(pl.multiple_of(half * n_u, n_u), n_u)]
            ref[:, n_q + n_o + n_u :] = d_ref[pl.ds(pl.multiple_of(half * n_u, n_u), n_u), :].T

    return pl.pallas_call(
        body,
        in_specs=[pl.BlockSpec(memory_space=pltpu.SMEM)] + [pl.BlockSpec(memory_space=pltpu.VMEM)] * 4,
        out_shape=[jax.ShapeDtypeStruct((rows, width), BF)] * 2,
        compiler_params=pltpu.CompilerParams(vmem_limit_bytes=VMEM_LIMIT),
        cost_estimate=cost(2),
        name="split_weights",
    )(ids, w_qkv, w_out, w_up, w_down)


def up_forward(rows, weight, bias):
    count, depth = rows.shape
    width = weight.shape[1]
    step = min(256, width)

    def body(x_ref, w_ref, b_ref, act_ref, slope_ref):
        u = dot_nn(x_ref[...], w_ref[...]) + b_ref[...]
        square = u * u
        inner = u * (0.7978845608028654 + (0.7978845608028654 * 0.044715) * square)
        t = jnp.tanh(inner)
        half = 0.5 + 0.5 * t
        act_ref[...] = (u * half).astype(BF)
        rise = 0.7978845608028654 + (3 * 0.7978845608028654 * 0.044715) * square
        slope_ref[...] = (half + (0.5 * u) * (1.0 - t * t) * rise).astype(BF)

    tile = pl.BlockSpec((count, step), lambda i: (0, i))
    return pl.pallas_call(
        body,
        grid=(width // step,),
        in_specs=[
            pl.BlockSpec((count, depth), lambda i: (0, 0)),
            pl.BlockSpec((depth, step), lambda i: (0, i)),
            pl.BlockSpec((1, step), lambda i: (0, i)),
        ],
        out_specs=[tile, tile],
        out_shape=[jax.ShapeDtypeStruct((count, width), BF)] * 2,
        compiler_params=pltpu.CompilerParams(vmem_limit_bytes=VMEM_LIMIT),
        cost_estimate=cost(12),
        name="up_forward",
    )(rows, weight, bias)


def up_backward(cot_rows, weight, slope):
    count, depth = cot_rows.shape
    width = weight.shape[1]
    step = min(256, width)

    def body(x_ref, w_ref, slope_ref, out_ref, sum_ref):
        grad = (dot_nn(x_ref[...], w_ref[...]) * slope_ref[...].astype(F32)).astype(BF)
        out_ref[...] = grad
        sum_ref[...] = jnp.sum(grad.astype(F32), axis=0, keepdims=True)

    tile = pl.BlockSpec((count, step), lambda i: (0, i))
    return pl.pallas_call(
        body,
        grid=(width // step,),
        in_specs=[
            pl.BlockSpec((count, depth), lambda i: (0, 0)),
            pl.BlockSpec((depth, step), lambda i: (0, i)),
            tile,
        ],
        out_specs=[tile, pl.BlockSpec((1, step), lambda i: (0, i))],
        out_shape=[jax.ShapeDtypeStruct((count, width), BF), jax.ShapeDtypeStruct((1, width), F32)],
        compiler_params=pltpu.CompilerParams(vmem_limit_bytes=VMEM_LIMIT),
        cost_estimate=cost(10),
        name="up_backward",
    )(cot_rows, weight, slope)


def swap_blocks(values, bit, block):
    count = values.shape[1] // block
    return jnp.concatenate([values[:, (r ^ (1 << bit)) * block : ((r ^ (1 << bit)) + 1) * block] for r in range(count)], axis=1)


def add_chips_moves(total):
    if chip_bits() != 2:
        return []
    far = lambda v: lax.ppermute(v, "dp", [(i, i ^ 6) for i in range(lax.axis_size("dp"))])
    return [(by_bit(1), total), (by_bit(2), total), (far, total)]


def add_chips(total, got, block):
    if chip_bits() == 2:
        terms = [total, *got]
        vectors = functools.reduce(jnp.add, [t[:8, r * block : (r + 1) * block] for r, t in enumerate(terms)])
        vectors = jnp.pad(vectors, ((0, 0), (0, total.shape[1] - block)))
        return jnp.concatenate([vectors, functools.reduce(jnp.add, [t[8:] for t in terms])], axis=0)
    for bit in range(chip_bits()):
        got = swap_bit(total, bit + 1)
        total = total + jnp.concatenate([swap_blocks(got[:8], bit, block), got[8:]], axis=0)
    return total


def local(
    hidden_in,
    ln1_gain,
    ln1_bias,
    qkv_weight,
    qkv_bias,
    out_weight,
    out_bias,
    ln2_gain,
    ln2_bias,
    up_weight,
    up_bias,
    down_weight,
    down_bias,
    cotangent,
):
    dp = lax.axis_size("dp")
    size = lax.axis_size("tensor")
    index = lax.axis_index("dp")
    core = index % 2
    chip = index // 2
    tensor = lax.axis_index("tensor")
    keeps = core == tensor % 2
    chips = dp // 2
    tokens, d_model = hidden_in.shape
    block = d_model // chips
    heads_here = qkv_weight.shape[1] // (3 * HD)
    pair = heads_here // 2
    rows = qkv_weight.shape[0]
    mixed = block % 128 == 0
    ids = jnp.stack([chip, core, tensor, keeps.astype(jnp.int32)]).astype(jnp.int32)
    small = ln1_gain.shape[0]
    plan = Plan(dp, size, small, d_model, heads_here, qkv_bias.shape[1], up_bias.shape[0], up_bias.shape[1])

    def relative(values):
        if mixed:
            return values
        return jnp.concatenate(
            [lax.dynamic_slice_in_dim(values, (chip ^ r) * block, block, 1) for r in range(chips)], axis=1
        )

    wide = [qkv_weight.shape[1] // 2, out_weight.shape[0] // 2, up_weight.shape[1] // 2, down_weight.shape[0] // 2]
    pack = wide[0]
    if mixed:
        own, give = split_weights(ids, qkv_weight, out_weight, up_weight, down_weight)
    else:
        w_q = qkv_weight.reshape(rows, 2, pair, 3, HD).transpose(0, 1, 3, 2, 4).reshape(rows, 2, 3 * pair * HD)
        parts = [w_q] + [w.reshape(rows, 2, -1) for w in (out_weight.T, up_weight, down_weight.T)]
        loc = jnp.concatenate(parts, axis=2).transpose(1, 0, 2)
        own = lax.dynamic_index_in_dim(loc, core, 0, keepdims=False)
        give = lax.dynamic_index_in_dim(loc, 1 - core, 0, keepdims=False)
    packed = jnp.concatenate(
        [v.reshape(-1) for v in (ln1_gain, ln1_bias, out_bias, ln2_gain, ln2_bias, down_bias, qkv_bias, up_bias)]
    )
    packed = jnp.pad(packed, (0, pack - packed.shape[0])).reshape(1, pack)
    slot = jnp.arange(16)[:, None]
    extra = jnp.where(slot == core * size + tensor, packed, jnp.zeros_like(packed))
    other = swap_core(give)
    extra = extra + swap_core(extra)
    piece = both_halves(own, other, core)
    at = [0]
    for w in wide:
        at.append(at[-1] + w)
    extra = jnp.pad(extra, ((0, 0), (0, at[2] - pack)))
    piece_q = jnp.concatenate([piece[:, : at[2]], extra], axis=0)
    piece_u, piece_d = piece[:, at[2] : at[3]], piece[:, at[3] :]
    block_rows = piece.shape[0]
    split = block_rows // 2

    hidden, cot = relative(hidden_in), relative(cotangent)
    got_q = exchange(*along_tensor(piece_q))
    (hidden_low,) = rows_low(chips, mixed, ids, hidden, False)
    cot_low, cot_sums = rows_low(chips, mixed, ids, cot, True)
    *got_q, hidden_low, cot_low = tie(*got_q, hidden_low, cot_low)
    line_q = gather_line(piece_q, wide[:2], got_q, 16)
    line_q, piece_u = tie(line_q, piece_u)
    near = gather_near(line_q)
    swapped_in = swap_pair(hidden_low)
    got = exchange(*near, *along_tensor(piece_u))
    near_q, got_u = got[: len(near)], got[len(near) :]
    here_in, z_one = rows_first(chips, mixed, ids, hidden, swapped_in)
    far = gather_far(near_q, split)
    got = exchange(*far, (swap_pair, cot_low), (swap_core, z_one))
    far_q, swapped_cot, other_one = got[: len(far)], got[-2], got[-1]
    seq_one = both_halves(z_one, other_one, core)

    *got_u, swapped_cot = tie(*got_u, swapped_cot)
    line_u = gather_line(piece_u, wide[2:3], got_u)
    near = gather_near(line_u)
    line_u, piece_d = tie(line_u, piece_d)
    near_u = exchange(*near) if near else ()
    got_d = exchange(*along_tensor(piece_d))
    here_cot = jnp.where(keeps, cot_low, swapped_cot)
    cot_rows = jnp.concatenate([here_cot, swap_core(here_cot)], axis=0)

    parts = gathered(line_q, near_q, far_q, split)
    w_qkv, w_out_t = join_chips(parts, wide[:2], block_rows)
    table = jnp.stack([low[block_rows - split :, :pack] for _, low in parts])[:, : 2 * size]
    vec, b_qkv, b_up = spread_small(plan, ids, table.reshape(chips * 2 * size, pack))
    head_ids = ((tensor + jnp.arange(size)) % size)[:, None] * heads_here + core * pair + jnp.arange(pair)[None]
    slopes = jnp.exp2(-8.0 * (head_ids + 1).astype(F32) / H)
    rows_one = (seq_one.astype(F32) * vec[0:1] + vec[1:2]).astype(BF)
    qkv = (dot_nn(rows_one, w_qkv) + b_qkv).astype(BF)
    context, lse = attend(qkv, slopes, 0, size, got_d[0])
    own, give = core_rows(context, core)
    far_u = exchange(*gather_far(near_u, split)) if near_u else ()
    line_d = gather_line(piece_d, wide[3:], got_d)
    got_here = swap_core(dot_nt(give, w_out_t).astype(BF))
    here = (dot_nt(own, w_out_t) + got_here.astype(F32)).astype(BF)
    near_d = exchange(*gather_near(line_d)) if near_u else ()
    (w_up,) = join_chips(gathered(line_u, near_u, far_u, split), wide[2:3], block_rows)
    residual, norm_two = rows_mid(ids, here_in, here, vec)
    norm_other = swap_core(norm_two)
    rows_two = jnp.concatenate([norm_two, norm_other], axis=0)
    active, slope = up_forward(rows_two, w_up, b_up)
    far_d = exchange(*gather_far(near_d, split)) if near_d else ()
    g_down_t = dot_tn(cot_rows, active).astype(BF)
    (w_down_t,) = join_chips(gathered(line_d, near_d, far_d, split), wide[3:], block_rows)

    moves = scatter_far(block_rows, g_down_t)
    far_gd = exchange(*moves) if moves else ()
    grad_pre, grad_b_up = up_backward(cot_rows, w_down_t, slope)
    *far_gd, grad_pre = tie(*far_gd, grad_pre)
    moves = scatter_near(block_rows, far_gd, g_down_t)
    near_gd = exchange(*moves) if moves else ()
    got_two = swap_core(dot_nt(grad_pre[tokens:], w_up).astype(BF))
    own_two = dot_nt(grad_pre[:tokens], w_up)
    g_up = dot_tn(rows_two, grad_pre).astype(BF)
    grad_mid, mid_low, mid_sums = rows_mid_back(chips, mixed, ids, cot, swapped_cot, residual, own_two, got_two, vec)
    other_mid = swap_core(mid_low)
    moves = scatter_far(block_rows, g_up)
    far_gu = exchange(*moves) if moves else ()
    active, mid_low = tie(active, mid_low)
    got_down = swap_core(dot_nt(active[tokens:], w_down_t).astype(BF))
    own_down = dot_nt(active[:tokens], w_down_t)
    out_here, out_low = rows_out(ids, residual, own_down, got_down, vec)
    output = rows_home(chips, mixed, ids, out_here, swap_pair(out_low))
    mid_rows = both_halves(mid_low, other_mid, core)
    grad_context = dot_nn(mid_rows, w_out_t).astype(BF)
    g_out_t = dot_tn(mid_rows, context).astype(BF)
    dq, cols = attend_back(qkv, slopes, lse, grad_context, 0, size, g_out_t)
    cols = cols.reshape(1, -1)
    vec_t = jnp.pad(vec[:8].T, ((0, 0), (0, 120)))
    g_q, one_sums = qkv_grads(seq_one, dq, w_qkv, 0, cols, vec_t)

    mid_sums = jnp.concatenate([mid_sums[:3], one_sums[:2], mid_sums[5:]], axis=0)
    riding = chip_bits() == 2
    both = pack + wide[1]
    extra = pack_rows(plan, ids, both, mid_sums, cot_sums, cols, grad_b_up) if riding else None
    got = tie(*near_gd, *far_gu, g_q)
    near_gd, far_gu, g_q = got[: len(near_gd)], got[len(near_gd) : -1], got[-1]
    moves = scatter_near(block_rows, far_gu, g_up)
    n = len(moves)
    moves = moves + scatter_far(block_rows, g_q, g_out_t, extra=extra)
    blocks_d = cut_blocks(scattered(block_rows, near_gd, g_down_t))
    got = exchange(*moves, *scatter_tensor(blocks_d))
    near_gu, far_q, turn_gd = got[:n], got[n : 2 * n], got[2 * n :]
    *far_q, dq = tie(*far_q, dq)
    own, give = core_rows(dq, core)
    got_one = swap_core(dot_nt(give, w_qkv).astype(BF))
    own_one = dot_nt(own, w_qkv)
    grad_here, grad_low = rows_first_back(ids, here_in, grad_mid, own_one, got_one, vec)
    moves = scatter_near(block_rows, far_q, g_q, g_out_t, extra=extra)
    blocks_u = cut_blocks(scattered(block_rows, near_gu, g_up))
    got = exchange(*moves, *scatter_tensor(blocks_u))
    near_q, turn_gu = got[: len(moves)], got[len(moves) :]
    line = scattered(block_rows, near_q, g_q, g_out_t, extra=extra)
    main = line[:block_rows]
    blocks = [
        jnp.concatenate(parts, axis=1)
        for parts in zip(cut_blocks(main[:, : size * pack]), cut_blocks(main[:, size * pack :]))
    ]
    if riding:
        blocks = [jnp.concatenate(parts, axis=0) for parts in zip(blocks, cut_blocks(line[block_rows:]))]
    turn_q = exchange(*scatter_tensor(blocks))
    swapped = swap_pair(grad_low)
    grad_in = rows_home(chips, mixed, ids, grad_here, swapped)
    keep_d, give_d = core_rows(scatter_total(blocks_d, turn_gd), core)
    keep_u, give_u = core_rows(scatter_total(blocks_u, turn_gu), core)
    back_d, back_u = exchange((swap_core, give_d), (swap_core, give_u))
    sum_up, sum_down = by_core(keep_u, back_u, core), by_core(keep_d, back_d, core)
    total_q = scatter_total(blocks, turn_q)
    keep_q, give_q = core_rows(total_q[:block_rows], core)
    back_q = swap_core(jnp.concatenate([give_q, total_q[block_rows:]], axis=0))
    sum_both = by_core(keep_q, back_q[: block_rows // 2], core)
    if riding:
        small_rows = total_q[block_rows:] + back_q[block_rows // 2 :]
        mine = lax.dynamic_index_in_dim(small_rows, core, 0, keepdims=False)
        vector_sums = [mine[i * small : (i + 1) * small] for i in range(6)]
        start = 6 * small
        sum_b_qkv = mine[start : start + qkv_bias.size].reshape(qkv_bias.shape)
        start += qkv_bias.size
        sum_b_up = mine[start : start + up_bias.size].reshape(up_bias.shape)
    else:
        total = pack_small(plan, ids, mid_sums, cot_sums, cols, grad_b_up)
        total = add_chips(total + swap_core(total), (), block)
        for bit in range((size - 1).bit_length()):
            total = total + lax.ppermute(total, "tensor", [(i, i ^ (1 << bit)) for i in range(size)])
        vector_sums, sum_b_qkv, sum_b_up = own_small(plan, total, index, tensor)
    sum_qkv, sum_out = sum_both[:, :, :pack], sum_both[:, :, pack:]

    sum_w_qkv = sum_qkv.reshape(rows, 2, 3, pair, HD).transpose(0, 1, 3, 2, 4).reshape(rows, -1)
    return (
        relative(output),
        relative(grad_in),
        vector_sums[0],
        vector_sums[1],
        sum_w_qkv,
        sum_b_qkv,
        sum_out.reshape(rows, -1).T,
        vector_sums[2],
        vector_sums[3],
        vector_sums[4],
        sum_up.reshape(rows, -1),
        sum_b_up,
        sum_down.reshape(rows, -1).T,
        vector_sums[5],
    )


def solution(mesh):
    both = P(("dp", "tensor"))
    wide = P(("dp", "tensor"), None)
    split, turned = P("dp", "tensor"), P("tensor", "dp")
    return jax.shard_map(
        local,
        mesh=mesh,
        in_specs=(wide, both, both, split, turned, turned, both, both, both, split, turned, turned, both, wide),
        out_specs=(wide, wide, both, both, split, turned, turned, both, both, both, split, turned, turned, both),
        check_vma=False,
    )
```

```python
import functools

import jax
import jax.numpy as jnp
from jax import lax
from jax.experimental import pallas as pl
from jax.experimental.pallas import tpu as pltpu
from jax.sharding import PartitionSpec as P

H = 16
HD = 64
FF = 4096
SEQ_LEN = 1024
EPSILON = 1e-05
MASKED = -1e30
BF = jnp.bfloat16
F32 = jnp.float32


def gelu_tanh(values):
    inner = 0.7978845608028654 * (values + 0.044715 * values * values * values)
    return 0.5 * values * (1.0 + jnp.tanh(inner))


def dot_nn(left, right):
    return lax.dot_general(left, right, (((1,), (0,)), ((), ())), preferred_element_type=F32)


def dot_tn(left, right):
    return lax.dot_general(left, right, (((0,), (0,)), ((), ())), preferred_element_type=F32)


def dot_nt(left, right):
    return lax.dot_general(left, right, (((1,), (1,)), ((), ())), preferred_element_type=F32)


def swap_bit(values, bit):
    size = lax.axis_size("dp")
    return lax.ppermute(values, "dp", [(i, i ^ (1 << bit)) for i in range(size)])


def swap_core(values):
    return swap_bit(values, 0)


def from_tensor(values, step):
    size = lax.axis_size("tensor")
    return lax.ppermute(values, "tensor", [(i, (i - step) % size) for i in range(size)])


def swap_pair(values):
    dp, tensor = lax.axis_size("dp"), lax.axis_size("tensor")
    pairs = []
    for d in range(dp):
        for t in range(tensor):
            if d % 2 != t % 2:
                pairs.append((d * tensor + t, (d ^ 1) * tensor + (t ^ 1)))
    return lax.ppermute(values, ("dp", "tensor"), pairs)


def chip_bits():
    return (lax.axis_size("dp") // 2).bit_length() - 1


def tie(*values):
    return lax.optimization_barrier(values)


def gather_line(piece, widths, turned, extra_rows=0):
    rows = piece.shape[0] - extra_rows
    turned = [piece] + list(turned)
    cols, at = [], 0
    for width in widths:
        cols += [t[:rows, at : at + width] for t in turned]
        at += width
    line = jnp.concatenate(cols, axis=1)
    if extra_rows:
        added = functools.reduce(jnp.add, [t[rows:] for t in turned])
        added = jnp.pad(added, ((0, 0), (0, line.shape[1] - added.shape[1])))
        line = jnp.concatenate([line, added], axis=0)
    return line


def exchange(*moves):
    values = lax.optimization_barrier(tuple(v for _, v in moves))
    return lax.optimization_barrier(tuple(move(v) for (move, _), v in zip(moves, values)))


def by_bit(bit):
    return functools.partial(swap_bit, bit=bit)


def by_tensor(step):
    return functools.partial(from_tensor, step=step)


def along_tensor(piece):
    return [(by_tensor(k), piece) for k in range(1, lax.axis_size("tensor"))]


def gather_near(line):
    return [(by_bit(1), line), (by_bit(2), line)] if chip_bits() == 2 else []


def gather_far(near, split):
    return [(by_bit(2), near[0][:split]), (by_bit(1), near[1][split:])] if chip_bits() == 2 else []


def gathered(line, near, far, split):
    if chip_bits() == 2:
        return [[v[:split], v[split:]] for v in (line, *near)] + [list(far)]
    held = line[None]
    for bit in range(chip_bits()):
        held = jnp.concatenate([held, swap_bit(held, bit + 1)], axis=0)
    return [[held[r, :split], held[r, split:]] for r in range(held.shape[0])]


def join_chips(got, widths, rows):
    size = lax.axis_size("tensor")
    out, at = [], 0
    for width in widths:
        cut = slice(at, at + size * width)
        out.append(jnp.concatenate([part for top, low in got for part in (top[:, cut], low[: rows - rows // 2, cut])]))
        at += size * width
    return out


def take(grads, low, high):
    return jnp.concatenate([g[low:high] for g in grads], axis=1) if len(grads) > 1 else grads[0][low:high]


def low_half(rows, r, grads, extra):
    low = take(grads, r * rows + rows // 2, (r + 1) * rows)
    return low if extra is None else jnp.concatenate([low, extra[r * 16 : (r + 1) * 16]], axis=0)


def scatter_far(rows, *grads, extra=None):
    if chip_bits() != 2:
        return []
    return [(by_bit(2), take(grads, 3 * rows, 3 * rows + rows // 2)), (by_bit(1), low_half(rows, 3, grads, extra))]


def scatter_near(rows, far, *grads, extra=None):
    if chip_bits() != 2:
        return []
    split = rows // 2
    top = (take(grads, rows, rows + split).astype(F32) + far[0].astype(F32)).astype(BF)
    low = (low_half(rows, 2, grads, extra).astype(F32) + far[1].astype(F32)).astype(BF)
    return [
        (by_bit(1), jnp.concatenate([top, low_half(rows, 1, grads, extra)], axis=0)),
        (by_bit(2), jnp.concatenate([take(grads, 2 * rows, 2 * rows + split), low], axis=0)),
    ]


def scattered(rows, near, *grads, extra=None):
    if chip_bits() == 2:
        own = jnp.concatenate([take(grads, 0, rows // 2), low_half(rows, 0, grads, extra)], axis=0)
        return own.astype(F32) + near[0].astype(F32) + near[1].astype(F32)
    grad = take(grads, 0, grads[0].shape[0])
    held = grad.reshape(-1, rows, grad.shape[1])
    for bit in range(chip_bits())[::-1]:
        half = held.shape[0] // 2
        got = swap_bit(held[half:], bit + 1)
        held = (held[:half].astype(F32) + got.astype(F32)).astype(BF)
    return held[0].astype(F32)


def scatter_tensor(blocks):
    size = lax.axis_size("tensor")
    return [(by_tensor(size - k), blocks[k].astype(BF)) for k in range(1, size)]


def cut_blocks(line):
    size = lax.axis_size("tensor")
    width = line.shape[1] // size
    return [line[:, k * width : (k + 1) * width] for k in range(size)]


def scatter_total(blocks, got):
    return functools.reduce(jnp.add, [part.astype(F32) for part in (blocks[0], *got)])


def core_rows(values, core):
    half = values.shape[0] // 2
    keep = lax.dynamic_slice_in_dim(values, core * half, half, 0)
    return keep, lax.dynamic_slice_in_dim(values, (1 - core) * half, half, 0)


def by_core(keep, back, core):
    return jnp.where(core == 0, jnp.stack([keep, back], 1), jnp.stack([back, keep], 1))


def both_halves(mine, other, core):
    return jnp.concatenate([jnp.where(core == 0, mine, other), jnp.where(core == 0, other, mine)], axis=0)


BLOCK_Q = 256


def cost(microseconds):
    return pl.CostEstimate(flops=int(microseconds * 1.1e9), bytes_accessed=int(microseconds * 1e6), transcendentals=0)


def biased_pair(q, k, slope_ref, group, head):
    seq = k.shape[0]
    lane = lax.broadcasted_iota(jnp.int32, (1, 2 * HD), 1)
    mine = (lane >= head * HD) & (lane < (head + 1) * HD)
    slot = lane & (HD - 1)
    bias = slope_ref[group, head] * lax.broadcasted_iota(jnp.int32, (seq, 2 * HD), 0).astype(F32)
    high = bias.astype(BF)
    rest = bias - high.astype(F32)
    middle = rest.astype(BF)
    low = (rest - middle.astype(F32)).astype(BF)
    zero = jnp.zeros_like(k)
    extra = jnp.where(slot == 0, high, jnp.where(slot == 1, middle, jnp.where(slot == 2, low, zero)))
    ones = jnp.where(slot < 3, 1.0, 0.0).astype(BF)
    return jnp.where(mine, q, jnp.broadcast_to(ones, q.shape)), jnp.where(mine, k, extra), mine


def below_diagonal(size):
    keys = lax.broadcasted_iota(jnp.int32, (size, size), 0)
    return keys <= lax.broadcasted_iota(jnp.int32, (size, size), 1)


def attend_kernel(start, slope_ref, qkv_ref, *refs):
    ctx_ref, lse_ref = refs[-2:]
    group = pl.program_id(0) + start
    wide = 2 * HD
    seq = qkv_ref.shape[0]
    size = min(BLOCK_Q, seq)
    q = qkv_ref[:, :wide] * BF(HD**-0.5)
    k = qkv_ref[:, wide : 2 * wide]
    v_t = qkv_ref[:, 2 * wide :].T
    heads = [biased_pair(q, k, slope_ref, group, h) for h in range(2)]
    seen = below_diagonal(size)
    for i in range(seq // size):
        lo, hi = i * size, (i + 1) * size
        outs = []
        for h, (qh, kh, _) in enumerate(heads):
            s = dot_nt(kh[:hi], qh[lo:hi])
            last = jnp.where(seen, s[lo:], MASKED)
            top = jnp.max(last, axis=0, keepdims=True)
            if i:
                top = jnp.maximum(top, jnp.max(s[:lo], axis=0, keepdims=True))
            e = jnp.exp(last - top)
            total = jnp.sum(e, axis=0, keepdims=True)
            e = e.astype(BF)
            if i:
                e0 = jnp.exp(s[:lo] - top)
                total = total + jnp.sum(e0, axis=0, keepdims=True)
                e = jnp.concatenate([e0.astype(BF), e], axis=0)
            o_t = dot_nn(v_t[h * HD : (h + 1) * HD, :hi], e)
            outs.append(o_t * (1.0 / total))
            lse_ref[0, h : h + 1, lo:hi] = top + jnp.log(total)
        ctx_ref[lo:hi, :] = jnp.concatenate(outs, axis=0).T.astype(BF)


def attend(qkv, slopes, first, groups, *earlier):
    seq = qkv.shape[0]
    wide = 2 * HD
    return pl.pallas_call(
        functools.partial(attend_kernel, first),
        grid=(groups,),
        in_specs=[
            pl.BlockSpec(memory_space=pltpu.SMEM),
            pl.BlockSpec((seq, 3 * wide), lambda g: (0, g + first)),
        ]
        + [pl.BlockSpec(memory_space=pl.ANY)] * len(earlier),
        out_specs=[
            pl.BlockSpec((seq, wide), lambda g: (0, g)),
            pl.BlockSpec((1, 2, seq), lambda g: (g, 0, 0)),
        ],
        out_shape=[
            jax.ShapeDtypeStruct((seq, groups * wide), BF),
            jax.ShapeDtypeStruct((groups, 2, seq), F32),
        ],
        compiler_params=pltpu.CompilerParams(vmem_limit_bytes=48 * 1024 * 1024),
        cost_estimate=cost(9),
        name="attend",
    )(slopes, qkv, *earlier)


def attend_back_kernel(start, slope_ref, qkv_ref, grad_ref, lse_ref, *refs):
    out_ref, bias_ref, dk_ref, dv_ref = refs[-4:]
    group = pl.program_id(0) + start
    wide = 2 * HD
    seq = qkv_ref.shape[0]
    size = min(BLOCK_Q, seq)
    q = qkv_ref[:, :wide] * BF(HD**-0.5)
    k = qkv_ref[:, wide : 2 * wide]
    v = qkv_ref[:, 2 * wide :]
    k_t = k.T
    zero = jnp.zeros_like(q)
    heads = [biased_pair(q, k, slope_ref, group, h) for h in range(2)]
    clean = [jnp.where(mine, q, zero) for _, _, mine in heads]
    grads = [jnp.where(mine, grad_ref[...], zero) for _, _, mine in heads]
    seen = below_diagonal(size)
    dk_ref[...] = jnp.zeros_like(dk_ref)
    dv_ref[...] = jnp.zeros_like(dv_ref)
    bias_q = jnp.zeros((1, wide), F32)
    for i in range(seq // size):
        lo, hi = i * size, (i + 1) * size
        outs = []
        for h, (qh, kh, _) in enumerate(heads):
            s = dot_nt(kh[:hi], qh[lo:hi])
            lse = lse_ref[0, h : h + 1, lo:hi]
            p = jnp.exp(jnp.where(seen, s[lo:], MASKED) - lse)
            if i:
                p = jnp.concatenate([jnp.exp(s[:lo] - lse), p], axis=0)
            dp = dot_nt(v[:hi], grads[h][lo:hi])
            inner = jnp.sum(p * dp, axis=0, keepdims=True)
            ds = (p * (dp - inner)).astype(BF)
            dk_ref[:hi, :] += dot_nn(ds, clean[h][lo:hi])
            dv_ref[:hi, :] += dot_nn(p.astype(BF), grads[h][lo:hi])
            outs.append(dot_nn(k_t[h * HD : (h + 1) * HD, :hi], ds))
        dq = (jnp.concatenate(outs, axis=0).T * HD**-0.5).astype(BF)
        bias_q = bias_q + jnp.sum(dq.astype(F32), axis=0, keepdims=True)
        out_ref[lo:hi, :wide] = dq
    dk = dk_ref[...].astype(BF)
    out_ref[:, wide : 2 * wide] = dk
    dv = dv_ref[...].astype(BF)
    out_ref[:, 2 * wide :] = dv
    bias_ref[0, :, :wide] = bias_q
    bias_ref[0, :, wide : 2 * wide] = jnp.sum(dk.astype(F32), axis=0, keepdims=True)
    bias_ref[0, :, 2 * wide :] = jnp.sum(dv.astype(F32), axis=0, keepdims=True)


def attend_back(qkv, slopes, lse, grad_ctx, first, groups, *earlier):
    seq = qkv.shape[0]
    wide = 2 * HD
    return pl.pallas_call(
        functools.partial(attend_back_kernel, first),
        grid=(groups,),
        in_specs=[
            pl.BlockSpec(memory_space=pltpu.SMEM),
            pl.BlockSpec((seq, 3 * wide), lambda g: (0, g + first)),
            pl.BlockSpec((seq, wide), lambda g: (0, g + first)),
            pl.BlockSpec((1, 2, seq), lambda g: (g, 0, 0)),
        ]
        + [pl.BlockSpec(memory_space=pl.ANY)] * len(earlier),
        out_specs=[
            pl.BlockSpec((seq, 3 * wide), lambda g: (0, g)),
            pl.BlockSpec((1, 1, 3 * wide), lambda g: (g, 0, 0)),
        ],
        out_shape=[
            jax.ShapeDtypeStruct((seq, groups * 3 * wide), BF),
            jax.ShapeDtypeStruct((groups, 1, 3 * wide), F32),
        ],
        scratch_shapes=[pltpu.VMEM((seq, wide), F32), pltpu.VMEM((seq, wide), F32)],
        compiler_params=pltpu.CompilerParams(vmem_limit_bytes=48 * 1024 * 1024),
        cost_estimate=cost(11),
        name="attend_back",
    )(slopes, qkv, grad_ctx, lse, *earlier)


VMEM_LIMIT = 48 * 1024 * 1024


def read_mixed(ref, ids_ref, chips, mixed):
    if not mixed:
        return ref[...]
    block = ref.shape[1] // chips
    parts = [ref[:, pl.ds(pl.multiple_of((ids_ref[0] ^ r) * block, block), block)] for r in range(chips)]
    return jnp.concatenate(parts, axis=1)


def write_mixed(ref, values, ids_ref, chips, mixed):
    if not mixed:
        ref[...] = values
        return
    block = ref.shape[1] // chips
    for r in range(chips):
        ref[:, pl.ds(pl.multiple_of((ids_ref[0] ^ r) * block, block), block)] = values[:, r * block : (r + 1) * block]


def centre(x):
    mean_row = jnp.mean(x, axis=1, keepdims=True)
    centred = x - mean_row
    inv = lax.rsqrt(jnp.mean(centred * centred, axis=1, keepdims=True) + EPSILON)
    return centred * inv, inv


def norm_back(grad, gain, z, inv):
    g = grad * gain
    mean_g = jnp.mean(g, axis=1, keepdims=True)
    mean_gz = jnp.mean(g * z, axis=1, keepdims=True)
    return inv * (g - mean_g - z * mean_gz)


def add_sums(ref, rows):
    @pl.when(pl.program_id(0) == 0)
    def _():
        ref[...] = jnp.zeros_like(ref)

    for i, row in enumerate(rows):
        ref[i : i + 1, :] += jnp.sum(row, axis=0, keepdims=True)


def row_call(body, name, ids, rows, wholes, outs, sums):
    tokens, width = rows[0].shape
    step = min(128, tokens)
    tile = pl.BlockSpec((step, width), lambda i: (i, 0))
    one = pl.BlockSpec((8, width), lambda i: (0, 0))
    shapes = [jax.ShapeDtypeStruct((tokens, width), t) for t in outs]
    if sums:
        shapes.append(jax.ShapeDtypeStruct((8, width), F32))
    moved = sum(r.size * r.dtype.itemsize for r in rows) + sum(tokens * width * jnp.dtype(t).itemsize for t in outs)
    return pl.pallas_call(
        body,
        grid=(tokens // step,),
        in_specs=[pl.BlockSpec(memory_space=pltpu.SMEM)] + [tile] * len(rows) + [one] * len(wholes),
        out_specs=[tile] * len(outs) + ([one] if sums else []),
        out_shape=shapes,
        compiler_params=pltpu.CompilerParams(vmem_limit_bytes=VMEM_LIMIT),
        cost_estimate=cost(3),
        name=name,
    )(ids, *rows, *wholes)


def chosen(own, swapped_ref, ids_ref):
    return jnp.where(ids_ref[3] == 1, own, swapped_ref[...].astype(F32))


def rows_low(chips, mixed, ids, values, sums):
    def body(ids_ref, x_ref, low_ref, *sum_refs):
        x = read_mixed(x_ref, ids_ref, chips, mixed)
        low_ref[...] = x.astype(BF)
        if sums:
            add_sums(sum_refs[0], [x])

    return row_call(body, "rows_low", ids, [values], [], [BF], sums)


def rows_first(chips, mixed, ids, hidden, swapped):
    def body(ids_ref, x_ref, swapped_ref, here_ref, z_ref):
        x = chosen(read_mixed(x_ref, ids_ref, chips, mixed), swapped_ref, ids_ref)
        here_ref[...] = x
        z_ref[...] = centre(x)[0].astype(BF)

    return row_call(body, "rows_first", ids, [hidden, swapped], [], [F32, BF], False)


def rows_mid(ids, hidden, added, vec):
    def body(ids_ref, x_ref, added_ref, vec_ref, res_ref, norm_ref):
        res = x_ref[...] + added_ref[...].astype(F32) + vec_ref[2:3, :]
        res_ref[...] = res
        norm_ref[...] = (centre(res)[0] * vec_ref[3:4, :] + vec_ref[4:5, :]).astype(BF)

    return row_call(body, "rows_mid", ids, [hidden, added], [vec], [F32, BF], False)


def rows_out(ids, residual, own, got, vec):
    def body(ids_ref, res_ref, own_ref, got_ref, vec_ref, out_ref, low_ref):
        out = res_ref[...] + (own_ref[...] + got_ref[...].astype(F32)) + vec_ref[5:6, :]
        out_ref[...] = out
        low_ref[...] = out.astype(BF)

    return row_call(body, "rows_out", ids, [residual, own, got], [vec], [F32, BF], False)


def rows_mid_back(chips, mixed, ids, cot, swapped, residual, own, got, vec):
    def body(ids_ref, cot_ref, swapped_ref, res_ref, own_ref, got_ref, vec_ref, grad_ref, low_ref, sum_ref):
        z, inv = centre(res_ref[...])
        grad = own_ref[...] + got_ref[...].astype(F32)
        above = chosen(read_mixed(cot_ref, ids_ref, chips, mixed), swapped_ref, ids_ref)
        mid = above + norm_back(grad, vec_ref[3:4, :], z, inv)
        grad_ref[...] = mid
        low_ref[...] = mid.astype(BF)
        add_sums(sum_ref, [grad * z, grad, mid])

    return row_call(body, "rows_mid_back", ids, [cot, swapped, residual, own, got], [vec], [F32, BF], True)


def rows_first_back(ids, hidden, grad_mid, own, got, vec):
    def body(ids_ref, x_ref, mid_ref, own_ref, got_ref, vec_ref, out_ref, low_ref):
        z, inv = centre(x_ref[...])
        out = mid_ref[...] + norm_back(own_ref[...] + got_ref[...].astype(F32), vec_ref[0:1, :], z, inv)
        out_ref[...] = out
        low_ref[...] = out.astype(BF)

    return row_call(body, "rows_first_back", ids, [hidden, grad_mid, own, got], [vec], [F32, BF], False)


def rows_home(chips, mixed, ids, here, swapped):
    def body(ids_ref, here_ref, swapped_ref, out_ref):
        write_mixed(out_ref, chosen(here_ref[...], swapped_ref, ids_ref), ids_ref, chips, mixed)

    return row_call(body, "rows_home", ids, [here, swapped], [], [F32], False)[0]


class Plan:
    def __init__(self, dp, size, small, d_model, heads, qb, ups, ub):
        self.dp, self.size, self.small, self.d_model = dp, size, small, d_model
        self.heads, self.qb, self.ups, self.ub = heads, qb, ups, ub
        self.chips = dp // 2
        self.pair = heads // 2
        self.n_q = size * 3 * self.pair * HD
        self.n_u = size * (ups // 2) * ub * dp
        self.used = 6 * small + heads * qb + ups * ub

    def vector(self, which, n):
        owner = n // self.small
        t = owner % self.size
        c = (owner // self.size) % 2
        r = owner // (2 * self.size)
        return r, c, t, which * self.small + n % self.small

    def query(self, n, chip, core, tensor):
        per = 3 * self.pair * HD
        part = (n % per) // (self.pair * HD)
        head = (n % (self.pair * HD)) // HD
        b = n % HD + jnp.where(part == 2, HD, 0)
        d = b // self.qb
        place = 6 * self.small + (core * self.pair + head) * self.qb + b % self.qb
        place = jnp.where(part == 1, -1, place)
        return chip ^ (d // 2), d % 2, (tensor + n // per) % self.size, place

    def up(self, n, chip, core, tensor):
        row_len = self.ub * self.dp
        per = (self.ups // 2) * row_len
        row = (n % per) // row_len
        d = (n % row_len) // self.ub
        place = 6 * self.small + self.heads * self.qb + (core * (self.ups // 2) + row) * self.ub + n % self.ub
        return chip ^ (d // 2), d % 2, (tensor + n // per) % self.size, place


def spread_small(plan, ids, table):
    count, pack = table.shape

    def body(ids_ref, table_ref, vec_ref, bq_ref, bu_ref):
        chip, core, tensor = ids_ref[0], ids_ref[1], ids_ref[2]

        def pick(where_, n):
            col = lax.broadcasted_iota(jnp.int32, (1, n), 1)
            r, c, t, place = where_(col)
            hot = lax.broadcasted_iota(jnp.int32, (pack, n), 0) == place
            got = dot_nn(table_ref[...], jnp.where(hot, 1.0, 0.0).astype(BF))
            row = (r * 2 + c) * plan.size + t
            return jnp.sum(
                jnp.where(lax.broadcasted_iota(jnp.int32, (count, n), 0) == row, got, 0.0), axis=0, keepdims=True
            )

        for v in range(6):
            vec_ref[v : v + 1, :] = pick(functools.partial(plan.vector, v), plan.d_model)
        vec_ref[6:8, :] = jnp.zeros((2, plan.d_model), F32)
        bq_ref[...] = pick(lambda n: plan.query(n, chip, core, tensor), plan.n_q)
        bu_ref[...] = pick(lambda n: plan.up(n, chip, core, tensor), plan.n_u)

    return pl.pallas_call(
        body,
        in_specs=[pl.BlockSpec(memory_space=pltpu.SMEM), pl.BlockSpec(memory_space=pltpu.VMEM)],
        out_shape=[
            jax.ShapeDtypeStruct((8, plan.d_model), F32),
            jax.ShapeDtypeStruct((1, plan.n_q), F32),
            jax.ShapeDtypeStruct((1, plan.n_u), F32),
        ],
        compiler_params=pltpu.CompilerParams(vmem_limit_bytes=VMEM_LIMIT),
        cost_estimate=cost(2),
        name="spread_small",
    )(ids, table)


def pack_small(plan, ids, mid_sums, cot_sums, bias_q, bias_u):
    size = plan.size
    width = plan.d_model
    per_q, per_u = plan.n_q // size, plan.n_u // size

    def body(ids_ref, mid_ref, cot_ref, bq_ref, bu_ref, out_ref):
        core, tensor = ids_ref[1], ids_ref[2]
        out_ref[...] = jnp.zeros_like(out_ref)
        out_ref[0:2, :] = mid_ref[3:5, :]
        out_ref[2:3, :] = mid_ref[2:3, :]
        out_ref[3:5, :] = mid_ref[0:2, :]
        out_ref[5:6, :] = cot_ref[0:1, :]
        at = 8
        for ref, per in ((bq_ref, per_q), (bu_ref, per_u)):
            x = ref[...]
            turned = x
            for t in range(1, size):
                moved = jnp.concatenate([x[:, (size - t) * per :], x[:, : (size - t) * per]], axis=1)
                turned = jnp.where(tensor == t, moved, turned)
            for c in range(2):
                put = jnp.where(core == c, turned, 0.0)
                for lo in range(0, put.shape[1], width):
                    part = put[:, lo : lo + width]
                    out_ref[at : at + 1, : part.shape[1]] = part
                    at += 1

    lines = 8 + 2 * (-(-plan.n_q // width) - (-plan.n_u // width))
    return pl.pallas_call(
        body,
        in_specs=[pl.BlockSpec(memory_space=pltpu.SMEM)] + [pl.BlockSpec(memory_space=pltpu.VMEM)] * 4,
        out_shape=jax.ShapeDtypeStruct((-(-lines // 8) * 8, width), F32),
        compiler_params=pltpu.CompilerParams(vmem_limit_bytes=VMEM_LIMIT),
        cost_estimate=cost(1),
        name="pack_small",
    )(ids, mid_sums, cot_sums, bias_q, bias_u)


def pack_rows(plan, ids, width, mid_sums, cot_sums, bias_q, bias_u):
    size, chips = plan.size, plan.chips

    def body(ids_ref, mid_ref, cot_ref, bq_ref, bu_ref, out_ref):
        chip, core, tensor = ids_ref[0], ids_ref[1], ids_ref[2]

        def put(where_, values):
            n = values.shape[1]
            r, c, t, place = where_(lax.broadcasted_iota(jnp.int32, (1, n), 1))
            hot = lax.broadcasted_iota(jnp.int32, (width, n), 0) == place
            row = (r * 2 + c) * size + (t - tensor + size) % size
            at = lax.broadcasted_iota(jnp.int32, (chips * 2 * size, n), 0) == row
            return dot_nt(jnp.where(at, values, 0.0).astype(BF), jnp.where(hot, 1.0, 0.0).astype(BF))

        rows = [mid_ref[3:4, :], mid_ref[4:5, :], mid_ref[2:3, :], mid_ref[0:1, :], mid_ref[1:2, :], cot_ref[0:1, :]]
        total = put(lambda n: plan.query(n, chip, core, tensor), bq_ref[...])
        total = total + put(lambda n: plan.up(n, chip, core, tensor), bu_ref[...])
        for v, row in enumerate(rows):
            total = total + put(functools.partial(plan.vector, v), row)
        for r in range(chips):
            lines = [
                jnp.concatenate([total[(r * 2 + c) * size + k :][:1] for k in range(size)], axis=1) for c in range(2)
            ]
            lines.append(jnp.zeros((14, size * width), F32))
            out_ref[r * 16 : (r + 1) * 16, :] = jnp.concatenate(lines, axis=0).astype(BF)

    return pl.pallas_call(
        body,
        in_specs=[pl.BlockSpec(memory_space=pltpu.SMEM)] + [pl.BlockSpec(memory_space=pltpu.VMEM)] * 4,
        out_shape=jax.ShapeDtypeStruct((chips * 16, size * width), BF),
        compiler_params=pltpu.CompilerParams(vmem_limit_bytes=VMEM_LIMIT),
        cost_estimate=cost(2),
        name="pack_rows",
    )(ids, mid_sums, cot_sums, bias_q, bias_u)


def own_small(plan, total, index, tensor):
    size, width = plan.size, plan.d_model
    n_q, n_u = -(-plan.n_q // width), -(-plan.n_u // width)
    vectors = lax.dynamic_slice_in_dim(total[:6], (index % 2 * size + tensor) * plan.small, plan.small, 1)
    q = total[8 : 8 + 2 * n_q].reshape(2, -1)[:, : plan.n_q].reshape(2, size, 3, plan.pair, HD)
    q = lax.dynamic_index_in_dim(q, tensor, 1, keepdims=False)
    q = jnp.stack([q[:, 0], q[:, 2]], axis=2).reshape(plan.heads, 2 * HD)
    q = lax.dynamic_slice_in_dim(q, index * plan.qb, plan.qb, 1)
    u = total[8 + 2 * n_q : 8 + 2 * (n_q + n_u)].reshape(2, -1)[:, : plan.n_u].reshape(2, size, plan.ups // 2, -1)
    u = lax.dynamic_index_in_dim(u, tensor, 1, keepdims=False).reshape(plan.ups, -1)
    u = lax.dynamic_slice_in_dim(u, index * plan.ub, plan.ub, 1)
    return [vectors[i] for i in range(6)], q, u


def qkv_grads(seq_one, grad_qkv, w_qkv, part, colsum, vec_t, *earlier):
    seq, d_model = seq_one.shape
    width = grad_qkv.shape[1]
    step = min(256, d_model)

    def body(z_ref, grad_ref, w_ref, col_ref, vec_ref, *refs):
        out_ref, sum_ref = refs[-2:]
        g = lax.dot_general(z_ref[...], grad_ref[...], (((0,), (0,)), ((), ())), preferred_element_type=F32)
        w = w_ref[...].astype(F32)
        col = col_ref[...]
        out_ref[...] = (g * vec_ref[:, 0:1] + vec_ref[:, 1:2] * col).astype(BF)
        gain = jnp.sum(g * w, axis=1, keepdims=True)
        shift = jnp.sum(w * col, axis=1, keepdims=True)
        lane = lax.broadcasted_iota(jnp.int32, (step, 128), 1)
        sum_ref[...] = jnp.where(lane == 0, gain, jnp.where(lane == 1, shift, 0.0)).T[:8]

    return pl.pallas_call(
        body,
        grid=(d_model // step,),
        in_specs=[
            pl.BlockSpec((seq, step), lambda i: (0, i)),
            pl.BlockSpec((seq, width), lambda i: (0, 0)),
            pl.BlockSpec((step, width), lambda i: (i, part)),
            pl.BlockSpec((1, width), lambda i: (0, 0)),
            pl.BlockSpec((step, 128), lambda i: (i, 0)),
        ]
        + [pl.BlockSpec(memory_space=pl.ANY)] * len(earlier),
        out_specs=[pl.BlockSpec((step, width), lambda i: (i, 0)), pl.BlockSpec((8, step), lambda i: (0, i))],
        out_shape=[jax.ShapeDtypeStruct((d_model, width), BF), jax.ShapeDtypeStruct((8, d_model), F32)],
        compiler_params=pltpu.CompilerParams(vmem_limit_bytes=VMEM_LIMIT),
        cost_estimate=cost(5),
        name="qkv_grads",
    )(seq_one, grad_qkv, w_qkv, colsum, vec_t, *earlier)


def split_weights(ids, w_qkv, w_out, w_up, w_down):
    rows = w_qkv.shape[0]
    n_q, n_o, n_u = w_qkv.shape[1] // 2, w_out.shape[0] // 2, w_up.shape[1] // 2
    pair = n_q // (3 * HD)
    width = n_q + n_o + 2 * n_u

    def body(ids_ref, q_ref, o_ref, u_ref, d_ref, mine_ref, give_ref):
        core = ids_ref[1]
        for half, ref in ((core, mine_ref), (1 - core, give_ref)):
            x = q_ref[:, pl.ds(pl.multiple_of(half * n_q, n_q), n_q)]
            parts = [
                x[:, (h * 3 + p) * HD : (h * 3 + p + 1) * HD] for p in range(3) for h in range(pair)
            ]
            ref[:, :n_q] = jnp.concatenate(parts, axis=1)
            ref[:, n_q : n_q + n_o] = o_ref[pl.ds(pl.multiple_of(half * n_o, n_o), n_o), :].T
            ref[:, n_q + n_o : n_q + n_o + n_u] = u_ref[:, pl.ds(pl.multiple_of(half * n_u, n_u), n_u)]
            ref[:, n_q + n_o + n_u :] = d_ref[pl.ds(pl.multiple_of(half * n_u, n_u), n_u), :].T

    return pl.pallas_call(
        body,
        in_specs=[pl.BlockSpec(memory_space=pltpu.SMEM)] + [pl.BlockSpec(memory_space=pltpu.VMEM)] * 4,
        out_shape=[jax.ShapeDtypeStruct((rows, width), BF)] * 2,
        compiler_params=pltpu.CompilerParams(vmem_limit_bytes=VMEM_LIMIT),
        cost_estimate=cost(2),
        name="split_weights",
    )(ids, w_qkv, w_out, w_up, w_down)


def up_forward(rows, weight, bias):
    count, depth = rows.shape
    width = weight.shape[1]
    step = min(512, width)

    def body(x_ref, w_ref, b_ref, act_ref, slope_ref):
        u = dot_nn(x_ref[...], w_ref[...]) + b_ref[...]
        square = u * u
        inner = u * (0.7978845608028654 + (0.7978845608028654 * 0.044715) * square)
        t = jnp.tanh(inner)
        half = 0.5 + 0.5 * t
        act_ref[...] = (u * half).astype(BF)
        rise = 0.7978845608028654 + (3 * 0.7978845608028654 * 0.044715) * square
        slope_ref[...] = (half + (0.5 * u) * (1.0 - t * t) * rise).astype(BF)

    tile = pl.BlockSpec((count, step), lambda i: (0, i))
    return pl.pallas_call(
        body,
        grid=(width // step,),
        in_specs=[
            pl.BlockSpec((count, depth), lambda i: (0, 0)),
            pl.BlockSpec((depth, step), lambda i: (0, i)),
            pl.BlockSpec((1, step), lambda i: (0, i)),
        ],
        out_specs=[tile, tile],
        out_shape=[jax.ShapeDtypeStruct((count, width), BF)] * 2,
        compiler_params=pltpu.CompilerParams(vmem_limit_bytes=VMEM_LIMIT),
        cost_estimate=cost(12),
        name="up_forward",
    )(rows, weight, bias)


def up_backward(cot_rows, weight, slope):
    count, depth = cot_rows.shape
    width = weight.shape[1]
    step = min(512, width)

    def body(x_ref, w_ref, slope_ref, out_ref, sum_ref):
        grad = (dot_nn(x_ref[...], w_ref[...]) * slope_ref[...].astype(F32)).astype(BF)
        out_ref[...] = grad
        sum_ref[...] = jnp.sum(grad.astype(F32), axis=0, keepdims=True)

    tile = pl.BlockSpec((count, step), lambda i: (0, i))
    return pl.pallas_call(
        body,
        grid=(width // step,),
        in_specs=[
            pl.BlockSpec((count, depth), lambda i: (0, 0)),
            pl.BlockSpec((depth, step), lambda i: (0, i)),
            tile,
        ],
        out_specs=[tile, pl.BlockSpec((1, step), lambda i: (0, i))],
        out_shape=[jax.ShapeDtypeStruct((count, width), BF), jax.ShapeDtypeStruct((1, width), F32)],
        compiler_params=pltpu.CompilerParams(vmem_limit_bytes=VMEM_LIMIT),
        cost_estimate=cost(10),
        name="up_backward",
    )(cot_rows, weight, slope)


def swap_blocks(values, bit, block):
    count = values.shape[1] // block
    return jnp.concatenate([values[:, (r ^ (1 << bit)) * block : ((r ^ (1 << bit)) + 1) * block] for r in range(count)], axis=1)


def add_chips_moves(total):
    if chip_bits() != 2:
        return []
    far = lambda v: lax.ppermute(v, "dp", [(i, i ^ 6) for i in range(lax.axis_size("dp"))])
    return [(by_bit(1), total), (by_bit(2), total), (far, total)]


def add_chips(total, got, block):
    if chip_bits() == 2:
        terms = [total, *got]
        vectors = functools.reduce(jnp.add, [t[:8, r * block : (r + 1) * block] for r, t in enumerate(terms)])
        vectors = jnp.pad(vectors, ((0, 0), (0, total.shape[1] - block)))
        return jnp.concatenate([vectors, functools.reduce(jnp.add, [t[8:] for t in terms])], axis=0)
    for bit in range(chip_bits()):
        got = swap_bit(total, bit + 1)
        total = total + jnp.concatenate([swap_blocks(got[:8], bit, block), got[8:]], axis=0)
    return total


def local(
    hidden_in,
    ln1_gain,
    ln1_bias,
    qkv_weight,
    qkv_bias,
    out_weight,
    out_bias,
    ln2_gain,
    ln2_bias,
    up_weight,
    up_bias,
    down_weight,
    down_bias,
    cotangent,
):
    dp = lax.axis_size("dp")
    size = lax.axis_size("tensor")
    index = lax.axis_index("dp")
    core = index % 2
    chip = index // 2
    tensor = lax.axis_index("tensor")
    keeps = core == tensor % 2
    chips = dp // 2
    tokens, d_model = hidden_in.shape
    block = d_model // chips
    heads_here = qkv_weight.shape[1] // (3 * HD)
    pair = heads_here // 2
    rows = qkv_weight.shape[0]
    mixed = block % 128 == 0
    ids = jnp.stack([chip, core, tensor, keeps.astype(jnp.int32)]).astype(jnp.int32)
    small = ln1_gain.shape[0]
    plan = Plan(dp, size, small, d_model, heads_here, qkv_bias.shape[1], up_bias.shape[0], up_bias.shape[1])

    def relative(values):
        if mixed:
            return values
        return jnp.concatenate(
            [lax.dynamic_slice_in_dim(values, (chip ^ r) * block, block, 1) for r in range(chips)], axis=1
        )

    wide = [qkv_weight.shape[1] // 2, out_weight.shape[0] // 2, up_weight.shape[1] // 2, down_weight.shape[0] // 2]
    pack = wide[0]
    if mixed:
        own, give = split_weights(ids, qkv_weight, out_weight, up_weight, down_weight)
    else:
        w_q = qkv_weight.reshape(rows, 2, pair, 3, HD).transpose(0, 1, 3, 2, 4).reshape(rows, 2, 3 * pair * HD)
        parts = [w_q] + [w.reshape(rows, 2, -1) for w in (out_weight.T, up_weight, down_weight.T)]
        loc = jnp.concatenate(parts, axis=2).transpose(1, 0, 2)
        own = lax.dynamic_index_in_dim(loc, core, 0, keepdims=False)
        give = lax.dynamic_index_in_dim(loc, 1 - core, 0, keepdims=False)
    packed = jnp.concatenate(
        [v.reshape(-1) for v in (ln1_gain, ln1_bias, out_bias, ln2_gain, ln2_bias, down_bias, qkv_bias, up_bias)]
    )
    packed = jnp.pad(packed, (0, pack - packed.shape[0])).reshape(1, pack)
    slot = jnp.arange(16)[:, None]
    extra = jnp.where(slot == core * size + tensor, packed, jnp.zeros_like(packed))
    other = swap_core(give)
    extra = extra + swap_core(extra)
    piece = both_halves(own, other, core)
    at = [0]
    for w in wide:
        at.append(at[-1] + w)
    extra = jnp.pad(extra, ((0, 0), (0, at[2] - pack)))
    piece_q = jnp.concatenate([piece[:, : at[2]], extra], axis=0)
    piece_u, piece_d = piece[:, at[2] : at[3]], piece[:, at[3] :]
    block_rows = piece.shape[0]
    split = block_rows // 2

    hidden, cot = relative(hidden_in), relative(cotangent)
    got_q = exchange(*along_tensor(piece_q))
    (hidden_low,) = rows_low(chips, mixed, ids, hidden, False)
    cot_low, cot_sums = rows_low(chips, mixed, ids, cot, True)
    *got_q, hidden_low, cot_low = tie(*got_q, hidden_low, cot_low)
    line_q = gather_line(piece_q, wide[:2], got_q, 16)
    line_q, piece_u = tie(line_q, piece_u)
    near = gather_near(line_q)
    swapped_in = swap_pair(hidden_low)
    got = exchange(*near, *along_tensor(piece_u))
    near_q, got_u = got[: len(near)], got[len(near) :]
    here_in, z_one = rows_first(chips, mixed, ids, hidden, swapped_in)
    far = gather_far(near_q, split)
    got = exchange(*far, (swap_pair, cot_low), (swap_core, z_one))
    far_q, swapped_cot, other_one = got[: len(far)], got[-2], got[-1]
    seq_one = both_halves(z_one, other_one, core)

    *got_u, swapped_cot = tie(*got_u, swapped_cot)
    line_u = gather_line(piece_u, wide[2:3], got_u)
    near = gather_near(line_u)
    line_u, piece_d = tie(line_u, piece_d)
    near_u = exchange(*near) if near else ()
    got_d = exchange(*along_tensor(piece_d))
    here_cot = jnp.where(keeps, cot_low, swapped_cot)
    cot_rows = jnp.concatenate([here_cot, swap_core(here_cot)], axis=0)

    parts = gathered(line_q, near_q, far_q, split)
    w_qkv, w_out_t = join_chips(parts, wide[:2], block_rows)
    table = jnp.stack([low[block_rows - split :, :pack] for _, low in parts])[:, : 2 * size]
    vec, b_qkv, b_up = spread_small(plan, ids, table.reshape(chips * 2 * size, pack))
    head_ids = ((tensor + jnp.arange(size)) % size)[:, None] * heads_here + core * pair + jnp.arange(pair)[None]
    slopes = jnp.exp2(-8.0 * (head_ids + 1).astype(F32) / H)
    rows_one = (seq_one.astype(F32) * vec[0:1] + vec[1:2]).astype(BF)
    qkv = (dot_nn(rows_one, w_qkv) + b_qkv).astype(BF)
    context, lse = attend(qkv, slopes, 0, size, got_d[0])
    own, give = core_rows(context, core)
    far_u = exchange(*gather_far(near_u, split)) if near_u else ()
    line_d = gather_line(piece_d, wide[3:], got_d)
    got_here = swap_core(dot_nt(give, w_out_t).astype(BF))
    here = (dot_nt(own, w_out_t) + got_here.astype(F32)).astype(BF)
    near_d = exchange(*gather_near(line_d)) if near_u else ()
    (w_up,) = join_chips(gathered(line_u, near_u, far_u, split), wide[2:3], block_rows)
    residual, norm_two = rows_mid(ids, here_in, here, vec)
    norm_other = swap_core(norm_two)
    rows_two = jnp.concatenate([norm_two, norm_other], axis=0)
    active, slope = up_forward(rows_two, w_up, b_up)
    far_d = exchange(*gather_far(near_d, split)) if near_d else ()
    g_down_t = dot_tn(cot_rows, active).astype(BF)
    (w_down_t,) = join_chips(gathered(line_d, near_d, far_d, split), wide[3:], block_rows)

    moves = scatter_far(block_rows, g_down_t)
    far_gd = exchange(*moves) if moves else ()
    grad_pre, grad_b_up = up_backward(cot_rows, w_down_t, slope)
    *far_gd, grad_pre = tie(*far_gd, grad_pre)
    moves = scatter_near(block_rows, far_gd, g_down_t)
    near_gd = exchange(*moves) if moves else ()
    got_two = swap_core(dot_nt(grad_pre[tokens:], w_up).astype(BF))
    own_two = dot_nt(grad_pre[:tokens], w_up)
    g_up = dot_tn(rows_two, grad_pre).astype(BF)
    grad_mid, mid_low, mid_sums = rows_mid_back(chips, mixed, ids, cot, swapped_cot, residual, own_two, got_two, vec)
    other_mid = swap_core(mid_low)
    moves = scatter_far(block_rows, g_up)
    far_gu = exchange(*moves) if moves else ()
    active, mid_low = tie(active, mid_low)
    got_down = swap_core(dot_nt(active[tokens:], w_down_t).astype(BF))
    own_down = dot_nt(active[:tokens], w_down_t)
    out_here, out_low = rows_out(ids, residual, own_down, got_down, vec)
    output = rows_home(chips, mixed, ids, out_here, swap_pair(out_low))
    mid_rows = both_halves(mid_low, other_mid, core)
    grad_context = dot_nn(mid_rows, w_out_t).astype(BF)
    g_out_t = dot_tn(mid_rows, context).astype(BF)
    dq, cols = attend_back(qkv, slopes, lse, grad_context, 0, size, g_out_t)
    cols = cols.reshape(1, -1)
    vec_t = jnp.pad(vec[:8].T, ((0, 0), (0, 120)))
    g_q, one_sums = qkv_grads(seq_one, dq, w_qkv, 0, cols, vec_t)

    mid_sums = jnp.concatenate([mid_sums[:3], one_sums[:2], mid_sums[5:]], axis=0)
    riding = chip_bits() == 2
    both = pack + wide[1]
    extra = pack_rows(plan, ids, both, mid_sums, cot_sums, cols, grad_b_up) if riding else None
    got = tie(*near_gd, *far_gu, g_q)
    near_gd, far_gu, g_q = got[: len(near_gd)], got[len(near_gd) : -1], got[-1]
    moves = scatter_near(block_rows, far_gu, g_up)
    n = len(moves)
    moves = moves + scatter_far(block_rows, g_q, g_out_t, extra=extra)
    blocks_d = cut_blocks(scattered(block_rows, near_gd, g_down_t))
    got = exchange(*moves, *scatter_tensor(blocks_d))
    near_gu, far_q, turn_gd = got[:n], got[n : 2 * n], got[2 * n :]
    *far_q, dq = tie(*far_q, dq)
    own, give = core_rows(dq, core)
    got_one = swap_core(dot_nt(give, w_qkv).astype(BF))
    own_one = dot_nt(own, w_qkv)
    grad_here, grad_low = rows_first_back(ids, here_in, grad_mid, own_one, got_one, vec)
    moves = scatter_near(block_rows, far_q, g_q, g_out_t, extra=extra)
    blocks_u = cut_blocks(scattered(block_rows, near_gu, g_up))
    got = exchange(*moves, *scatter_tensor(blocks_u))
    near_q, turn_gu = got[: len(moves)], got[len(moves) :]
    line = scattered(block_rows, near_q, g_q, g_out_t, extra=extra)
    main = line[:block_rows]
    blocks = [
        jnp.concatenate(parts, axis=1)
        for parts in zip(cut_blocks(main[:, : size * pack]), cut_blocks(main[:, size * pack :]))
    ]
    if riding:
        blocks = [jnp.concatenate(parts, axis=0) for parts in zip(blocks, cut_blocks(line[block_rows:]))]
    turn_q = exchange(*scatter_tensor(blocks))
    swapped = swap_pair(grad_low)
    grad_in = rows_home(chips, mixed, ids, grad_here, swapped)
    keep_d, give_d = core_rows(scatter_total(blocks_d, turn_gd), core)
    keep_u, give_u = core_rows(scatter_total(blocks_u, turn_gu), core)
    back_d, back_u = exchange((swap_core, give_d), (swap_core, give_u))
    sum_up, sum_down = by_core(keep_u, back_u, core), by_core(keep_d, back_d, core)
    total_q = scatter_total(blocks, turn_q)
    keep_q, give_q = core_rows(total_q[:block_rows], core)
    back_q = swap_core(jnp.concatenate([give_q, total_q[block_rows:]], axis=0))
    sum_both = by_core(keep_q, back_q[: block_rows // 2], core)
    if riding:
        small_rows = total_q[block_rows:] + back_q[block_rows // 2 :]
        mine = lax.dynamic_index_in_dim(small_rows, core, 0, keepdims=False)
        vector_sums = [mine[i * small : (i + 1) * small] for i in range(6)]
        start = 6 * small
        sum_b_qkv = mine[start : start + qkv_bias.size].reshape(qkv_bias.shape)
        start += qkv_bias.size
        sum_b_up = mine[start : start + up_bias.size].reshape(up_bias.shape)
    else:
        total = pack_small(plan, ids, mid_sums, cot_sums, cols, grad_b_up)
        total = add_chips(total + swap_core(total), (), block)
        for bit in range((size - 1).bit_length()):
            total = total + lax.ppermute(total, "tensor", [(i, i ^ (1 << bit)) for i in range(size)])
        vector_sums, sum_b_qkv, sum_b_up = own_small(plan, total, index, tensor)
    sum_qkv, sum_out = sum_both[:, :, :pack], sum_both[:, :, pack:]

    sum_w_qkv = sum_qkv.reshape(rows, 2, 3, pair, HD).transpose(0, 1, 3, 2, 4).reshape(rows, -1)
    return (
        relative(output),
        relative(grad_in),
        vector_sums[0],
        vector_sums[1],
        sum_w_qkv,
        sum_b_qkv,
        sum_out.reshape(rows, -1).T,
        vector_sums[2],
        vector_sums[3],
        vector_sums[4],
        sum_up.reshape(rows, -1),
        sum_b_up,
        sum_down.reshape(rows, -1).T,
        vector_sums[5],
    )


def solution(mesh):
    both = P(("dp", "tensor"))
    wide = P(("dp", "tensor"), None)
    split, turned = P("dp", "tensor"), P("tensor", "dp")
    return jax.shard_map(
        local,
        mesh=mesh,
        in_specs=(wide, both, both, split, turned, turned, both, both, both, split, turned, turned, both, wide),
        out_specs=(wide, wide, both, both, split, turned, turned, both, both, both, split, turned, turned, both),
        check_vma=False,
    )
```
